256 devices in a mesh: node: 8 (over x, core), cut: 32 (over y, z).
Axes of the slice: x: 4, y: 4, z: 8, core: 2. Of those that a mesh axis runs over, the one named last changes fastest.
Arguments:
- trial_states: bfloat16 [2048, 4096], P('cut'), may hold values from -6 to 6
- cut_slopes: bfloat16 [32, 4096, 4096], P('node', 'cut'), may hold values from -0.09375 to 0.09375
- cut_intercepts: float32 [32, 4096], P('node', 'cut'), may hold values from 0 to 3
- transition: float32 [32, 32], replicated, may hold values from 0.02 to 1
Outputs:
- expected_values: float32 [32, 64, 32], P('cut', 'node')
The draws below stay inside these ranges and needn't reach their ends.
All inputs are finite; a program needn't handle non-finite values.
Results may differ from the reference program's by a relative error of at most 0.0028.
Values may be sent and summed in bfloat16 or wider, within the bound.
A program may use at most 64 MiB of HBM per device.

```python
import math
import jax
import jax.numpy as jnp
from jax import lax

S = 4096
TRIAL_DEV = 64
NODES = 32
CUTS = 4096
TRIALS = 2048
N_CUT = 32


def block_levels(rng, extent, cuts, low, largest):
    gain = 1.0
    for dim, blocks in cuts:
        heights = jax.random.uniform(jax.random.fold_in(jax.random.fold_in(rng, 6), dim), (blocks,), jnp.float32, low / len(cuts), largest / len(cuts))
        gain = gain * jnp.repeat(jnp.exp(heights), extent[dim] // blocks).reshape((-1,) + (1,) * (len(extent) - 1 - dim))
    return gain


def normal_values(rng, dims, scale, reach, pieces=(), kind=jnp.bfloat16):
    factor_of = block_levels(rng, dims, pieces, -0.22, 0.18) if pieces else 1.0
    drawn = jax.random.normal(rng, dims, jnp.float32) * scale * factor_of
    return jnp.minimum(jnp.maximum(drawn, -reach), reach).astype(kind)


def setup_inputs(seed: int = 0) -> dict:
    streams_of = jax.random.split(jax.random.key(seed), 5)
    trial_states = normal_values(streams_of[0], (TRIALS, S), 1.0, 6.0, ((0, 32),))
    cut_slopes = normal_values(streams_of[1], (NODES, CUTS, S), S ** -0.5, 0.09375, ((0, 8), (1, 32)))
    cut_intercepts = jnp.clip(3.0 * jax.random.uniform(streams_of[2], (NODES, CUTS), jnp.float32) ** block_levels(streams_of[2], (NODES, CUTS), ((0, 8), (1, 32)), -0.2, 0.2), 0.0, 3.0)
    transition = jnp.clip(jnp.exp(jax.random.uniform(streams_of[3], (NODES, NODES), jnp.float32, math.log(0.02), math.log(1.0))), 0.02, 1.0)
    return dict(trial_states=trial_states, cut_slopes=cut_slopes, cut_intercepts=cut_intercepts, transition=transition)


def reference(trial_states, cut_slopes, cut_intercepts, transition):
    def valuate(operands):
        slope_rows, offsets = operands
        scores = jnp.dot(trial_states, slope_rows.T, preferred_element_type=jnp.float32) + offsets[None, :]
        return jnp.max(scores, axis=1)

    node_values = lax.map(valuate, (cut_slopes, cut_intercepts))
    mixing = transition / jnp.sum(transition, axis=1, keepdims=True)
    values = jnp.dot(node_values.T, mixing.T, precision=lax.Precision.HIGHEST, preferred_element_type=jnp.float32)
    return values.reshape(N_CUT, TRIAL_DEV, NODES)
```

```python
import functools

import jax
import jax.numpy as jnp
from jax import lax
from jax.experimental import pallas as pl
from jax.experimental.pallas import tpu as pltpu
from jax.sharding import PartitionSpec as P

MESH = pl.DeviceIdType.MESH

NY, NZ, NX = 4, 8, 4

FETCH = 2816

PZ, MZ, PY, MY = (0, 1), (0, -1), (1, 0), (-1, 0)
LINKS = (PZ, MZ, PY, MY)

CROSS = {
    PZ: [(0, 1), (0, 2), (0, 3), (2, 1), (0, 4), (2, 2), (2, 3), (1, 4)],
    MZ: [(0, -1), (0, -2), (0, -3), (2, -1), (2, -2), (2, -3), (2, 4)],
    PY: [(1, 0), (2, 0), (1, 1), (1, -1), (1, 2), (1, -2), (1, 3), (1, -3)],
    MY: [(-1, 0), (-1, 1), (-1, -1), (-1, 2), (-1, -2), (-1, 3), (-1, -3), (-1, 4)],
}
HALVES = (0, 1)


def wrap(o):
    return (o[0] % NY, o[1] % NZ)


def plan(window, span, delay):
    todo = {d: [(wrap(o), h) for o in order for h in HALVES] for d, order in CROSS.items()}
    here = {((0, 0), h) for h in HALVES}
    free = dict.fromkeys(LINKS, 0.0)
    flying = dict.fromkeys(LINKS, 0)
    arrivals = []

    def issue(now):
        sends = []
        for d in LINKS:
            for o, h in list(todo[d]):
                source = wrap((o[0] - d[0], o[1] - d[1]))
                if flying[d] < window and (source, h) in here:
                    todo[d].remove((o, h))
                    flying[d] += 1
                    free[d] = max(free[d], now) + span
                    arrivals.append((free[d] + delay, len(arrivals), d, o, h))
                    sends.append((source, h, d))
        return sends

    first = issue(0.0)
    turns = []
    while len(turns) < len(arrivals):
        now, _, d, o, h = sorted(arrivals)[len(turns)]
        here.add((o, h))
        flying[d] -= 1
        turns.append((o, h, issue(now)))
    return first, turns


FIRST, TURNS = plan(window=3, span=1.8, delay=2.5)
PLACE = {(0, 0): 0}
for o, h, _ in TURNS:
    if (o, 1 - h) in [t[:2] for t in TURNS[:TURNS.index((o, h, _))]]:
        PLACE[o] = len(PLACE)
ARRIVALS = sorted(PLACE, key=PLACE.get)
PIECES = 8
NEED = [1 + max(i for i, t in enumerate(TURNS) if PLACE[t[0]] < 8 * g + 8) for g in range(4)]
STEPS = 3 * PIECES


def handled(step):
    group, which = step // PIECES, step % PIECES
    if step < 0:
        return 0
    return NEED[group] + (NEED[min(group + 1, 3)] - NEED[group]) * which // PIECES


def kernel(
    trial_ref, slope_ref, offset_ref, trans_ref, out_ref,
    gath, slopes, offset, weights, icol, sums, part, got, nodev, vals,
    local_sem, swap_send, swap_recv, yz_send, yz_recv, x_send, x_recv, a_send, a_recv, b_send, b_recv,
):
    node = lax.axis_index("node")
    cut = lax.axis_index("cut")
    x, core = node // 2, node % 2
    y, z = cut // NZ, cut % NZ
    odd = x % 2
    sibling = x * 2 + 1 - core
    share = 1 - core
    width = trial_ref.shape[1]
    own_rows = slope_ref.shape[0]
    rows = gath.shape[1]
    hrows = rows // 2
    extra = width - FETCH
    fetch_at = pl.multiple_of(odd * extra, 128)
    mine_at = pl.multiple_of(odd * FETCH, 128)
    other_at = pl.multiple_of((1 - odd) * FETCH, 128)
    beside = {d: ((y + d[0] + NY) % NY) * NZ + (z + d[1] + NZ) % NZ for d in LINKS}

    def yz_copy(o, h, d):
        oc = wrap((o[0] + d[0], o[1] + d[1]))
        piece = (pl.ds(h * hrows, hrows), pl.ds(fetch_at, FETCH))
        source = gath.at[PLACE[o], *piece]
        if o == (0, 0):
            source = trial_ref.at[pl.ds(share * rows + h * hrows, hrows), pl.ds(fetch_at, FETCH)]
        return pltpu.make_async_remote_copy(
            src_ref=source, dst_ref=gath.at[PLACE[oc], *piece],
            send_sem=yz_send, recv_sem=yz_recv.at[PLACE[oc] - 1, h],
            device_id=(node, beside[d]), device_id_type=MESH,
        )

    def yz_arrived(o, h):
        ref = gath.at[PLACE[o], pl.ds(h * hrows, hrows), pl.ds(fetch_at, FETCH)]
        pltpu.make_async_copy(ref, ref, yz_recv.at[PLACE[o] - 1, h]).wait()

    def x_copy(o, h):
        ref = gath.at[PLACE[o], pl.ds(h * hrows, hrows), pl.ds(mine_at, extra)]
        to = ((x + (1 if h == 0 else NX - 1)) % NX) * 2 + core
        return pltpu.make_async_remote_copy(
            src_ref=ref, dst_ref=ref, send_sem=x_send, recv_sem=x_recv.at[PLACE[o] // 8],
            device_id=(to, cut), device_id_type=MESH,
        )

    def x_arrived(group):
        low = max(8 * group, 1)
        ref = gath.at[pl.ds(low, 8 * group + 8 - low), :, pl.ds(other_at, extra)]
        pltpu.make_async_copy(ref, ref, x_recv.at[group]).wait()

    def product(group, m, at, lanes):
        span = pl.ds(at, lanes)
        states = gath[pl.ds(8 * group, 8), :, span].reshape(8 * rows, lanes)
        return lax.dot_general(
            slopes[pl.ds(m * 256, 256), span], states, (((1,), (1,)), ((), ())),
            preferred_element_type=jnp.float32,
        )

    def compute(piece):
        group = lax.div(piece, PIECES)
        m = lax.rem(piece, PIECES // 2)

        @pl.when(lax.rem(piece, PIECES) < PIECES // 2)
        def _():
            sums[m] = product(group, m, fetch_at, FETCH)

        @pl.when(lax.rem(piece, PIECES) >= PIECES // 2)
        def _():
            add = icol[m]
            total = sums[m] + product(group, m, other_at, extra) + jnp.concatenate([add, add], axis=1)
            best = jnp.max(total.reshape(2, 128, 8 * rows), axis=1)
            part[2 * group, m] = best[:, 0:128]
            part[2 * group + 1, m] = best[:, 128:256]

    def finish():
        def whole(at, lanes):
            span = pl.ds(at, lanes)
            states = gath[pl.ds(24, 8), :, span].reshape(8 * rows, lanes)
            return lax.dot_general(
                slopes[:, span], states, (((1,), (1,)), ((), ())), preferred_element_type=jnp.float32
            )

        sums[...] = whole(fetch_at, FETCH).reshape(sums.shape)
        x_arrived(3)
        rest = whole(other_at, extra).reshape(sums.shape)
        for m in range(4):
            add = icol[m]
            total = sums[m] + rest[m] + jnp.concatenate([add, add], axis=1)
            best = jnp.max(total.reshape(2, 128, 8 * rows), axis=1)
            part[6, m] = best[:, 0:128]
            part[7, m] = best[:, 128:256]

    def tell(group):
        for i in range(max(8 * group, 1), 8 * group + 8):
            o = ARRIVALS[i]
            owner = ((y - o[0] + NY) % NY) * NZ + (z - o[1] + NZ) % NZ
            pltpu.make_async_remote_copy(
                src_ref=part.at[i // 4], dst_ref=got.at[i - 1], send_sem=a_send, recv_sem=a_recv,
                device_id=(node, owner), device_id_type=MESH,
            ).start()

    own = pltpu.make_async_copy(trial_ref.at[pl.ds(share * rows, rows)], gath.at[0], local_sem.at[0])
    load = pltpu.make_async_copy(slope_ref, slopes.at[pl.ds(core * own_rows, own_rows)], local_sem.at[1])
    load_offset = pltpu.make_async_copy(offset_ref, offset.at[core], local_sem.at[2])
    load_trans = pltpu.make_async_copy(trans_ref, weights, local_sem.at[3])
    swap = pltpu.make_async_remote_copy(
        src_ref=slope_ref, dst_ref=slopes.at[pl.ds(core * own_rows, own_rows)],
        send_sem=swap_send.at[0], recv_sem=swap_recv.at[0],
        device_id=(sibling, cut), device_id_type=MESH,
    )
    swap_offset = pltpu.make_async_remote_copy(
        src_ref=offset_ref, dst_ref=offset.at[core],
        send_sem=swap_send.at[1], recv_sem=swap_recv.at[1],
        device_id=(sibling, cut), device_id_type=MESH,
    )
    barrier = pltpu.get_barrier_semaphore()
    for d in LINKS:
        pl.semaphore_signal(barrier, inc=1, device_id=(node, beside[d]), device_id_type=MESH)
    for j in range(1, 8):
        pl.semaphore_signal(barrier, inc=1, device_id=((node + j) % 8, cut), device_id_type=MESH)
    own.start()
    load_offset.start()
    load_trans.start()
    pl.semaphore_wait(barrier, 11)

    for o, h, d in FIRST:
        yz_copy(o, h, d).start()
    swap_offset.start()
    swap.start()
    load.start()
    load_offset.wait()
    swap_offset.wait()
    for c in range(2):
        for n in range(4):
            line = jnp.broadcast_to(offset[c, n:n + 1, :], (128, 128))
            icol[2 * c + n // 2, pl.ds(n % 2 * 128, 128), :] = line.T

    def talk(k):
        for o, h, sends in TURNS[handled(k - 1):handled(k)]:
            yz_arrived(o, h)
            for send in sends:
                yz_copy(*send).start()
            x_copy(o, h).start()
        if k == 0:
            own.wait()
            load.wait()
            swap.wait()
        if k % PIECES == 0 and k > 0:
            tell(k // PIECES - 1)
        if k % PIECES == PIECES // 2:
            x_arrived(k // PIECES)

    def choose(step, low, high):
        if high - low == 1:
            talk(low)
            return
        mid = (low + high) // 2

        @pl.when(step < mid)
        def _():
            choose(step, low, mid)

        @pl.when(step >= mid)
        def _():
            choose(step, mid, high)

    def turn(step, carry):
        choose(step, 0, STEPS)
        compute(step)
        return carry

    lax.fori_loop(0, STEPS, turn, 0)
    talk(STEPS)
    finish()
    tell(3)

    for at, lanes, sem in ((fetch_at, FETCH, yz_send), (mine_at, extra, x_send)):
        ref = gath.at[pl.ds(0, len(ARRIVALS) - 1), :, pl.ds(at, lanes)]
        pltpu.make_async_copy(ref, ref, sem).wait()
    pltpu.make_async_copy(got, got, a_recv).wait()
    pltpu.make_async_copy(got, got, a_send).wait()
    best = None
    for q in range(4):
        tiles = [got[i - 1] for i in range(q, len(ARRIVALS), 4) if i > 0]
        if q == 0:
            tiles.append(part[0])
        top = functools.reduce(jnp.maximum, tiles)[:, :, q * rows:(q + 1) * rows]
        best = top if best is None else jnp.maximum(best, top)
    nodev[node, :, :, 0:rows] = best
    for j in range(4):
        to = 4 * share + j

        @pl.when(to != node)
        def _():
            pltpu.make_async_remote_copy(
                src_ref=nodev.at[node], dst_ref=nodev.at[node], send_sem=b_send, recv_sem=b_recv,
                device_id=(to, cut), device_id_type=MESH,
            ).start()

    load_trans.wait()
    trans = weights[...]
    mixing = trans / jnp.sum(trans, axis=1, keepdims=True)
    holder = 1 - node // 4
    keeps = holder == core

    @pl.when(keeps)
    def _():
        ref = nodev.at[pl.ds(0, 3)]
        pltpu.make_async_copy(ref, ref, b_recv).wait()
        pltpu.make_async_copy(ref, ref, b_send).wait()

    @pl.when(jnp.logical_not(keeps))
    def _():
        ref = nodev.at[pl.ds(0, 4)]
        pltpu.make_async_copy(ref, ref, b_recv).wait()
        pltpu.make_async_copy(ref, ref, b_send).wait()

    known = jnp.concatenate(
        [nodev[2 * i + holder, m, :, 0:rows] for i in range(NX) for m in range(4)], axis=0
    )
    vals[...] = lax.dot_general(
        known.T, mixing, (((1,), (1,)), ((), ())),
        precision=lax.Precision.HIGHEST, preferred_element_type=jnp.float32,
    )
    out_ref[0] = vals[pl.ds(pl.multiple_of((node % 4) * 8, 8), 8), :]


def per_device(trial_states, cut_slopes, cut_intercepts, transition):
    node_local, cut_local, width = cut_slopes.shape
    rows = trial_states.shape[0]
    nodes = transition.shape[0]
    slope_rows = cut_slopes.reshape(node_local * cut_local, width)
    count = len(ARRIVALS)
    sems = pltpu.SemaphoreType.DMA
    return pl.pallas_call(
        kernel,
        out_shape=jax.ShapeDtypeStruct((1, rows // 8, nodes), jnp.float32),
        in_specs=[pl.BlockSpec(memory_space=pltpu.HBM)] * 4,
        out_specs=pl.BlockSpec(memory_space=pltpu.VMEM),
        scratch_shapes=[
            pltpu.VMEM((count, rows // 2, width), jnp.bfloat16),
            pltpu.VMEM((2 * node_local * cut_local, width), jnp.bfloat16),
            pltpu.VMEM((2, node_local, cut_local), jnp.float32),
            pltpu.VMEM(transition.shape, jnp.float32),
            pltpu.VMEM((4, 2 * cut_local, 128), jnp.float32),
            pltpu.VMEM((4, 2 * cut_local, 4 * rows), jnp.float32),
            pltpu.VMEM((count // 4, 4, 2, 128), jnp.float32),
            pltpu.VMEM((count - 1, 4, 2, 128), jnp.float32),
            pltpu.VMEM((8, 4, 2, 128), jnp.float32),
            pltpu.VMEM((rows // 2, nodes), jnp.float32),
            sems((4,)),
            sems((2,)),
            sems((2,)),
            sems(()),
            sems((count - 1, 2)),
            sems(()),
            sems((count // 8,)),
            sems(()),
            sems(()),
            sems(()),
            sems(()),
        ],
        compiler_params=pltpu.CompilerParams(
            collective_id=0, has_side_effects=True, vmem_limit_bytes=40 * 1024 * 1024
        ),
        cost_estimate=pl.CostEstimate(
            flops=2 * 512 * 2048 * 4096, bytes_accessed=5 * 1024 * 1024, transcendentals=0
        ),
    )(*[
        pltpu.with_memory_space_constraint(v, pltpu.HBM)
        for v in (trial_states, slope_rows, cut_intercepts, transition)
    ])


def solution(mesh):
    return jax.shard_map(
        per_device,
        mesh=mesh,
        in_specs=(P("cut", None), P("node", "cut", None), P("node", "cut"), P()),
        out_specs=P("cut", "node", None),
        check_vma=False,
    )
```

```python
import functools

import jax
import jax.numpy as jnp
from jax import lax
from jax.experimental import pallas as pl
from jax.experimental.pallas import tpu as pltpu
from jax.sharding import PartitionSpec as P

MESH = pl.DeviceIdType.MESH

NY, NZ, NX = 4, 8, 4

TILE, OVER, MIDDLE = 128, 10, 12
FETCH = OVER + MIDDLE

PZ, MZ, PY, MY = (0, 1), (0, -1), (1, 0), (-1, 0)
LINKS = (PZ, MZ, PY, MY)

CROSS = {
    PZ: [(0, 1), (0, 2), (0, 3), (2, 1), (0, 4), (2, 2), (2, 3), (1, 4)],
    MZ: [(0, -1), (0, -2), (0, -3), (2, -1), (2, -2), (2, -3), (2, 4)],
    PY: [(1, 0), (2, 0), (1, 1), (1, -1), (1, 2), (1, -2), (1, 3), (1, -3)],
    MY: [(-1, 0), (-1, 1), (-1, -1), (-1, 2), (-1, -2), (-1, 3), (-1, -3), (-1, 4)],
}
PARTS = (0, 1)


def wrap(o):
    return (o[0] % NY, o[1] % NZ)


def plan(window, span, delay):
    todo = {d: [(wrap(o), h) for o in order for h in PARTS] for d, order in CROSS.items()}
    here = {((0, 0), h) for h in PARTS}
    free = dict.fromkeys(LINKS, 0.0)
    flying = dict.fromkeys(LINKS, 0)
    arrivals = []

    def issue(now):
        sends = []
        for d in LINKS:
            for o, h in list(todo[d]):
                source = wrap((o[0] - d[0], o[1] - d[1]))
                if flying[d] < window and (source, h) in here:
                    todo[d].remove((o, h))
                    flying[d] += 1
                    free[d] = max(free[d], now) + span
                    arrivals.append((free[d] + delay, len(arrivals), d, o, h))
                    sends.append((source, h, d))
        return sends

    first = issue(0.0)
    turns = []
    while len(turns) < len(arrivals):
        now, _, d, o, h = sorted(arrivals)[len(turns)]
        here.add((o, h))
        flying[d] -= 1
        turns.append((o, h, issue(now)))
    return first, turns


FIRST, TURNS = plan(window=3, span=1.8, delay=2.5)
PLACE = {(0, 0): 0}
for o, h, _ in TURNS:
    if (o, 1 - h) in [t[:2] for t in TURNS[:TURNS.index((o, h, _))]]:
        PLACE[o] = len(PLACE)
ARRIVALS = sorted(PLACE, key=PLACE.get)
PIECES = 8
NEED = [1 + max(i for i, t in enumerate(TURNS) if PLACE[t[0]] < 8 * g + 8) for g in range(4)]
STEPS = 3 * PIECES


def handled(step):
    group, which = step // PIECES, step % PIECES
    if step < 0:
        return 0
    return NEED[group] + (NEED[min(group + 1, 3)] - NEED[group]) * which // PIECES


def kernel(
    trial_ref, slope_ref, offset_ref, trans_ref, out_ref,
    gath, slopes, offset, weights, icol, sums, part, got, nodev, vals,
    local_sem, swap_send, swap_recv, yz_send, yz_recv, x_send, x_recv, a_send, a_recv, b_send, b_recv,
):
    node = lax.axis_index("node")
    cut = lax.axis_index("cut")
    x, core = node // 2, node % 2
    y, z = cut // NZ, cut % NZ
    odd = x % 2
    sibling = x * 2 + 1 - core
    share = 1 - core
    tiles = gath.shape[1]
    own_rows = slope_ref.shape[0]
    rows = gath.shape[2]
    fetch_at = odd * OVER
    mine_at = odd * FETCH
    other_at = (1 - odd) * FETCH
    beside = {d: ((y + d[0] + NY) % NY) * NZ + (z + d[1] + NZ) % NZ for d in LINKS}

    def part_of(o, h):
        return gath.at[PLACE[o], pl.ds(mine_at, OVER) if h == 0 else pl.ds(OVER, MIDDLE)]

    def yz_copy(o, h, d):
        oc = wrap((o[0] + d[0], o[1] + d[1]))
        return pltpu.make_async_remote_copy(
            src_ref=part_of(o, h), dst_ref=part_of(oc, h),
            send_sem=yz_send, recv_sem=yz_recv.at[PLACE[oc] - 1, h],
            device_id=(node, beside[d]), device_id_type=MESH,
        )

    def yz_arrived(o, h):
        ref = part_of(o, h)
        pltpu.make_async_copy(ref, ref, yz_recv.at[PLACE[o] - 1, h]).wait()

    def x_copy(o, way):
        ref = gath.at[PLACE[o], pl.ds(mine_at + way * (OVER // 2), OVER // 2)]
        to = ((x + (1 if way == 0 else NX - 1)) % NX) * 2 + core
        return pltpu.make_async_remote_copy(
            src_ref=ref, dst_ref=ref, send_sem=x_send, recv_sem=x_recv.at[PLACE[o] // 8],
            device_id=(to, cut), device_id_type=MESH,
        )

    def x_arrived(group):
        low = max(8 * group, 1)
        ref = gath.at[pl.ds(low, 8 * group + 8 - low), pl.ds(other_at, OVER)]
        pltpu.make_async_copy(ref, ref, x_recv.at[group]).wait()

    def product(group, at, count, low, size):
        left = [slopes[at + k, pl.ds(low, size), :] for k in range(count)]
        right = [gath[pl.ds(8 * group, 8), at + k].reshape(8 * rows, TILE) for k in range(count)]
        return lax.dot_general(
            jnp.concatenate(left, axis=1), jnp.concatenate(right, axis=1), (((1,), (1,)), ((), ())),
            preferred_element_type=jnp.float32,
        )

    def compute(piece):
        group = lax.div(piece, PIECES)
        m = lax.rem(piece, PIECES // 2)

        @pl.when(lax.rem(piece, PIECES) < PIECES // 2)
        def _():
            sums[m] = product(group, fetch_at, FETCH, m * 256, 256)

        @pl.when(lax.rem(piece, PIECES) >= PIECES // 2)
        def _():
            add = icol[m]
            total = sums[m] + product(group, other_at, OVER, m * 256, 256) + jnp.concatenate([add, add], axis=1)
            best = jnp.max(total.reshape(2, 128, 8 * rows), axis=1)
            part[2 * group, m] = best[:, 0:128]
            part[2 * group + 1, m] = best[:, 128:256]

    def finish():
        sums[...] = product(3, fetch_at, FETCH, 0, 2 * own_rows).reshape(sums.shape)
        x_arrived(3)
        rest = product(3, other_at, OVER, 0, 2 * own_rows).reshape(sums.shape)
        for m in range(4):
            add = icol[m]
            total = sums[m] + rest[m] + jnp.concatenate([add, add], axis=1)
            best = jnp.max(total.reshape(2, 128, 8 * rows), axis=1)
            part[6, m] = best[:, 0:128]
            part[7, m] = best[:, 128:256]

    def tell(group):
        for i in range(max(8 * group, 1), 8 * group + 8):
            o = ARRIVALS[i]
            owner = ((y - o[0] + NY) % NY) * NZ + (z - o[1] + NZ) % NZ
            pltpu.make_async_remote_copy(
                src_ref=part.at[i // 4], dst_ref=got.at[i - 1], send_sem=a_send, recv_sem=a_recv,
                device_id=(node, owner), device_id_type=MESH,
            ).start()

    def column(k):
        return pl.ds(pl.multiple_of(k * TILE, TILE), TILE)

    def own(k):
        return pltpu.make_async_copy(
            trial_ref.at[pl.ds(share * rows, rows), column(k)], gath.at[0, k], local_sem.at[0]
        )

    def load(k):
        return pltpu.make_async_copy(
            slope_ref.at[:, column(k)], slopes.at[k, pl.ds(core * own_rows, own_rows)], local_sem.at[1]
        )

    loaded = slopes.at[:, pl.ds(core * own_rows, own_rows)]
    load_offset = pltpu.make_async_copy(offset_ref, offset.at[core], local_sem.at[2])
    load_trans = pltpu.make_async_copy(trans_ref, weights, local_sem.at[3])
    swap = pltpu.make_async_remote_copy(
        src_ref=loaded, dst_ref=loaded, send_sem=swap_send.at[0], recv_sem=swap_recv.at[0],
        device_id=(sibling, cut), device_id_type=MESH,
    )
    swap_offset = pltpu.make_async_remote_copy(
        src_ref=offset_ref, dst_ref=offset.at[core],
        send_sem=swap_send.at[1], recv_sem=swap_recv.at[1],
        device_id=(sibling, cut), device_id_type=MESH,
    )
    barrier = pltpu.get_barrier_semaphore()
    for d in LINKS:
        pl.semaphore_signal(barrier, inc=1, device_id=(node, beside[d]), device_id_type=MESH)
    for j in range(1, 8):
        pl.semaphore_signal(barrier, inc=1, device_id=((node + j) % 8, cut), device_id_type=MESH)
    for k in range(tiles):
        own(k).start()
    load_offset.start()
    load_trans.start()
    pl.semaphore_wait(barrier, 11)
    pltpu.make_async_copy(gath.at[0], gath.at[0], local_sem.at[0]).wait()

    for o, h, d in FIRST:
        yz_copy(o, h, d).start()
    swap_offset.start()
    for k in range(tiles):
        load(k).start()
    load_offset.wait()
    swap_offset.wait()
    for c in range(2):
        for n in range(4):
            line = jnp.broadcast_to(offset[c, n:n + 1, :], (128, 128))
            icol[2 * c + n // 2, pl.ds(n % 2 * 128, 128), :] = line.T

    pltpu.make_async_copy(loaded, loaded, local_sem.at[1]).wait()
    swap.start()

    def talk(k):
        for o, h, sends in TURNS[handled(k - 1):handled(k)]:
            yz_arrived(o, h)
            for send in sends:
                yz_copy(*send).start()
            if h == 0:
                x_copy(o, 0).start()
                x_copy(o, 1).start()
        if k == 0:
            swap.wait()
        if k % PIECES == 0 and k > 0:
            tell(k // PIECES - 1)
        if k % PIECES == PIECES // 2:
            x_arrived(k // PIECES)

    def choose(step, low, high):
        if high - low == 1:
            talk(low)
            return
        mid = (low + high) // 2

        @pl.when(step < mid)
        def _():
            choose(step, low, mid)

        @pl.when(step >= mid)
        def _():
            choose(step, mid, high)

    def turn(step, carry):
        choose(step, 0, STEPS)
        compute(step)
        return carry

    lax.fori_loop(0, STEPS, turn, 0)
    talk(STEPS)
    finish()
    tell(3)

    for count, sem in ((FETCH, yz_send), (OVER, x_send)):
        ref = gath.at[pl.ds(0, len(ARRIVALS) - 1), pl.ds(0, count)]
        pltpu.make_async_copy(ref, ref, sem).wait()
    pltpu.make_async_copy(got, got, a_recv).wait()
    pltpu.make_async_copy(got, got, a_send).wait()
    best = None
    for q in range(4):
        tiles = [got[i - 1] for i in range(q, len(ARRIVALS), 4) if i > 0]
        if q == 0:
            tiles.append(part[0])
        top = functools.reduce(jnp.maximum, tiles)[:, :, q * rows:(q + 1) * rows]
        best = top if best is None else jnp.maximum(best, top)
    nodev[node, :, :, 0:rows] = best
    for j in range(4):
        to = 4 * share + j

        @pl.when(to != node)
        def _():
            pltpu.make_async_remote_copy(
                src_ref=nodev.at[node], dst_ref=nodev.at[node], send_sem=b_send, recv_sem=b_recv,
                device_id=(to, cut), device_id_type=MESH,
            ).start()

    load_trans.wait()
    trans = weights[...]
    mixing = trans / jnp.sum(trans, axis=1, keepdims=True)
    holder = 1 - node // 4
    keeps = holder == core

    @pl.when(keeps)
    def _():
        ref = nodev.at[pl.ds(0, 3)]
        pltpu.make_async_copy(ref, ref, b_recv).wait()
        pltpu.make_async_copy(ref, ref, b_send).wait()

    @pl.when(jnp.logical_not(keeps))
    def _():
        ref = nodev.at[pl.ds(0, 4)]
        pltpu.make_async_copy(ref, ref, b_recv).wait()
        pltpu.make_async_copy(ref, ref, b_send).wait()

    known = jnp.concatenate(
        [nodev[2 * i + holder, m, :, 0:rows] for i in range(NX) for m in range(4)], axis=0
    )
    vals[...] = lax.dot_general(
        known.T, mixing, (((1,), (1,)), ((), ())),
        precision=lax.Precision.HIGHEST, preferred_element_type=jnp.float32,
    )
    out_ref[0] = vals[pl.ds(pl.multiple_of((node % 4) * 8, 8), 8), :]


def per_device(trial_states, cut_slopes, cut_intercepts, transition):
    node_local, cut_local, width = cut_slopes.shape
    rows = trial_states.shape[0]
    nodes = transition.shape[0]
    slope_rows = cut_slopes.reshape(node_local * cut_local, width)
    count = len(ARRIVALS)
    sems = pltpu.SemaphoreType.DMA
    return pl.pallas_call(
        kernel,
        out_shape=jax.ShapeDtypeStruct((1, rows // 8, nodes), jnp.float32),
        in_specs=[pl.BlockSpec(memory_space=pltpu.HBM)] * 4,
        out_specs=pl.BlockSpec(memory_space=pltpu.VMEM),
        scratch_shapes=[
            pltpu.VMEM((count, width // TILE, rows // 2, TILE), jnp.bfloat16),
            pltpu.VMEM((width // TILE, 2 * node_local * cut_local, TILE), jnp.bfloat16),
            pltpu.VMEM((2, node_local, cut_local), jnp.float32),
            pltpu.VMEM(transition.shape, jnp.float32),
            pltpu.VMEM((4, 2 * cut_local, 128), jnp.float32),
            pltpu.VMEM((4, 2 * cut_local, 4 * rows), jnp.float32),
            pltpu.VMEM((count // 4, 4, 2, 128), jnp.float32),
            pltpu.VMEM((count - 1, 4, 2, 128), jnp.float32),
            pltpu.VMEM((8, 4, 2, 128), jnp.float32),
            pltpu.VMEM((rows // 2, nodes), jnp.float32),
            sems((4,)),
            sems((2,)),
            sems((2,)),
            sems(()),
            sems((count - 1, 2)),
            sems(()),
            sems((count // 8,)),
            sems(()),
            sems(()),
            sems(()),
            sems(()),
        ],
        compiler_params=pltpu.CompilerParams(
            collective_id=0, has_side_effects=True, vmem_limit_bytes=40 * 1024 * 1024
        ),
        cost_estimate=pl.CostEstimate(
            flops=2 * 512 * 2048 * 4096, bytes_accessed=5 * 1024 * 1024, transcendentals=0
        ),
    )(*[
        pltpu.with_memory_space_constraint(v, pltpu.HBM)
        for v in (trial_states, slope_rows, cut_intercepts, transition)
    ])


def solution(mesh):
    return jax.shard_map(
        per_device,
        mesh=mesh,
        in_specs=(P("cut", None), P("node", "cut", None), P("node", "cut"), P()),
        out_specs=P("cut", "node", None),
        check_vma=False,
    )
```

```python
import functools

import jax
import jax.numpy as jnp
from jax import lax
from jax.experimental import pallas as pl
from jax.experimental.pallas import tpu as pltpu
from jax.sharding import PartitionSpec as P

MESH = pl.DeviceIdType.MESH

NY, NZ, NX = 4, 8, 4

TILE, OVER, MIDDLE = 128, 10, 12
FETCH = OVER + MIDDLE

PZ, MZ, PY, MY = (0, 1), (0, -1), (1, 0), (-1, 0)
LINKS = (PZ, MZ, PY, MY)

CROSS = {
    PZ: [(0, 1), (0, 2), (0, 3), (2, 1), (0, 4), (2, 2), (2, 3), (1, 4)],
    MZ: [(0, -1), (0, -2), (0, -3), (2, -1), (2, -2), (2, -3), (2, 4)],
    PY: [(1, 0), (2, 0), (1, 1), (1, -1), (1, 2), (1, -2), (1, 3), (1, -3)],
    MY: [(-1, 0), (-1, 1), (-1, -1), (-1, 2), (-1, -2), (-1, 3), (-1, -3), (-1, 4)],
}
PARTS = (0, 1)


def wrap(o):
    return (o[0] % NY, o[1] % NZ)


def plan(window, span, delay):
    todo = {d: [(wrap(o), h) for o in order for h in PARTS] for d, order in CROSS.items()}
    here = {((0, 0), h) for h in PARTS}
    free = dict.fromkeys(LINKS, 0.0)
    flying = dict.fromkeys(LINKS, 0)
    arrivals = []

    def issue(now):
        sends = []
        for d in LINKS:
            for o, h in list(todo[d]):
                source = wrap((o[0] - d[0], o[1] - d[1]))
                if flying[d] < window and (source, h) in here:
                    todo[d].remove((o, h))
                    flying[d] += 1
                    free[d] = max(free[d], now) + span
                    arrivals.append((free[d] + delay, len(arrivals), d, o, h))
                    sends.append((source, h, d))
        return sends

    first = issue(0.0)
    turns = []
    while len(turns) < len(arrivals):
        now, _, d, o, h = sorted(arrivals)[len(turns)]
        here.add((o, h))
        flying[d] -= 1
        turns.append((o, h, issue(now)))
    return first, turns


FIRST, TURNS = plan(window=3, span=1.8, delay=2.5)
PLACE = {(0, 0): 0}
for o, h, _ in TURNS:
    if (o, 1 - h) in [t[:2] for t in TURNS[:TURNS.index((o, h, _))]]:
        PLACE[o] = len(PLACE)
ARRIVALS = sorted(PLACE, key=PLACE.get)
PIECES = 4
NEED = [1 + max(i for i, t in enumerate(TURNS) if PLACE[t[0]] < 8 * g + 8) for g in range(4)]
STEPS = 4 * PIECES


def handled(step):
    group, which = step // PIECES, step % PIECES
    if step < 0:
        return 0
    return NEED[group] + (NEED[min(group + 1, 3)] - NEED[group]) * which // PIECES


def kernel(
    trial_ref, slope_ref, offset_ref, trans_ref, out_ref,
    gath, slopes, offset, weights, sums, part, got, nodev, vals,
    local_sem, swap_send, swap_recv, yz_send, yz_recv, x_send, x_recv, a_send, a_recv, b_send, b_recv,
):
    node = lax.axis_index("node")
    cut = lax.axis_index("cut")
    x, core = node // 2, node % 2
    y, z = cut // NZ, cut % NZ
    odd = x % 2
    sibling = x * 2 + 1 - core
    share = 1 - core
    tiles = gath.shape[1]
    own_rows = slope_ref.shape[0]
    rows = gath.shape[2]
    fetch_at = odd * OVER
    mine_at = odd * FETCH
    other_at = (1 - odd) * FETCH
    beside = {d: ((y + d[0] + NY) % NY) * NZ + (z + d[1] + NZ) % NZ for d in LINKS}

    def part_of(o, h):
        return gath.at[PLACE[o], pl.ds(mine_at, OVER) if h == 0 else pl.ds(OVER, MIDDLE)]

    def yz_copy(o, h, d):
        oc = wrap((o[0] + d[0], o[1] + d[1]))
        return pltpu.make_async_remote_copy(
            src_ref=part_of(o, h), dst_ref=part_of(oc, h),
            send_sem=yz_send, recv_sem=yz_recv.at[PLACE[oc] - 1, h],
            device_id=(node, beside[d]), device_id_type=MESH,
        )

    def yz_arrived(o, h):
        ref = part_of(o, h)
        pltpu.make_async_copy(ref, ref, yz_recv.at[PLACE[o] - 1, h]).wait()

    def x_copy(o, way):
        ref = gath.at[PLACE[o], pl.ds(mine_at + way * (OVER // 2), OVER // 2)]
        to = ((x + (1 if way == 0 else NX - 1)) % NX) * 2 + core
        return pltpu.make_async_remote_copy(
            src_ref=ref, dst_ref=ref, send_sem=x_send, recv_sem=x_recv.at[PLACE[o] // 8],
            device_id=(to, cut), device_id_type=MESH,
        )

    def x_arrived(group):
        low = max(8 * group, 1)
        ref = gath.at[pl.ds(low, 8 * group + 8 - low), pl.ds(other_at, OVER)]
        pltpu.make_async_copy(ref, ref, x_recv.at[group]).wait()

    def product(group, at, count, owner):
        low = owner * own_rows
        left = [gath[pl.ds(8 * group, 8), at + k].reshape(8 * rows, TILE) for k in range(count)]
        right = [slopes[at + k, pl.ds(low, own_rows), :] for k in range(count)]
        return lax.dot_general(
            jnp.concatenate(left, axis=1), jnp.concatenate(right, axis=1), (((1,), (1,)), ((), ())),
            preferred_element_type=jnp.float32,
        )

    def compute(piece):
        group = lax.div(piece, PIECES)
        which = lax.rem(piece, PIECES)
        owner = lax.rem(core + which, 2)

        @pl.when(which < 2)
        def _():
            sums[owner] = product(group, fetch_at, FETCH, owner)

        @pl.when(which >= 2)
        def _():
            rest = product(group, other_at, OVER, owner)
            lane = lax.broadcasted_iota(jnp.int32, (8 * rows, TILE), 1)
            best = jnp.zeros((8 * rows, TILE), jnp.float32)
            for n in range(4):
                at = slice(n * 128, n * 128 + 128)
                total = sums[owner, :, at] + rest[:, at] + offset[owner, n:n + 1, :]
                best = jnp.where(lane == n, jnp.max(total, axis=1, keepdims=True), best)
            turned = best.T
            part[2 * group, owner] = turned[0:4, 0:128]
            part[2 * group + 1, owner] = turned[0:4, 128:256]

    def tell(group):
        for i in range(max(8 * group, 1), 8 * group + 8):
            o = ARRIVALS[i]
            owner = ((y - o[0] + NY) % NY) * NZ + (z - o[1] + NZ) % NZ
            pltpu.make_async_remote_copy(
                src_ref=part.at[i // 4], dst_ref=got.at[i - 1], send_sem=a_send, recv_sem=a_recv,
                device_id=(node, owner), device_id_type=MESH,
            ).start()

    def column(k):
        return pl.ds(pl.multiple_of(k * TILE, TILE), TILE)

    def own(k, sem):
        return pltpu.make_async_copy(
            trial_ref.at[pl.ds(share * rows, rows), column(k)], gath.at[0, k], sem
        )

    own_parts = ((mine_at, OVER, local_sem.at[0]), (OVER, MIDDLE, local_sem.at[4]), (other_at, OVER, local_sem.at[5]))

    def own_arrived(i):
        at, count, sem = own_parts[i]
        ref = gath.at[0, pl.ds(at, count)]
        pltpu.make_async_copy(ref, ref, sem).wait()

    def load(k):
        return pltpu.make_async_copy(
            slope_ref.at[:, column(k)], slopes.at[k, pl.ds(core * own_rows, own_rows)], local_sem.at[1]
        )

    loaded = slopes.at[:, pl.ds(core * own_rows, own_rows)]
    load_offset = pltpu.make_async_copy(offset_ref, offset.at[core], local_sem.at[2])
    load_trans = pltpu.make_async_copy(trans_ref, weights, local_sem.at[3])
    swap = pltpu.make_async_remote_copy(
        src_ref=loaded, dst_ref=loaded, send_sem=swap_send.at[0], recv_sem=swap_recv.at[0],
        device_id=(sibling, cut), device_id_type=MESH,
    )
    swap_offset = pltpu.make_async_remote_copy(
        src_ref=offset_ref, dst_ref=offset.at[core],
        send_sem=swap_send.at[1], recv_sem=swap_recv.at[1],
        device_id=(sibling, cut), device_id_type=MESH,
    )
    barrier = pltpu.get_barrier_semaphore()
    for d in LINKS:
        pl.semaphore_signal(barrier, inc=1, device_id=(node, beside[d]), device_id_type=MESH)
    for j in range(1, 8):
        pl.semaphore_signal(barrier, inc=1, device_id=((node + j) % 8, cut), device_id_type=MESH)
    for at, count, sem in own_parts:
        for k in range(count):
            own(at + k, sem).start()
    load_offset.start()
    load_trans.start()
    pl.semaphore_wait(barrier, 11)
    for part_sent in PARTS:
        own_arrived(part_sent)
        for o, h, d in FIRST:
            if h == part_sent:
                yz_copy(o, h, d).start()
    swap_offset.start()
    for k in range(tiles):
        load(k).start()
    pltpu.make_async_copy(loaded, loaded, local_sem.at[1]).wait()
    swap.start()

    def talk(k):
        for o, h, sends in TURNS[handled(k - 1):handled(k)]:
            yz_arrived(o, h)
            for send in sends:
                yz_copy(*send).start()
            if h == 0:
                x_copy(o, 0).start()
                x_copy(o, 1).start()
        if k == 0:
            own_arrived(2)
            load_offset.wait()
        if k == 1:
            swap_offset.wait()
            swap.wait()
        if k % PIECES == 0 and k > 0:
            tell(k // PIECES - 1)
        if k % PIECES == PIECES // 2:
            x_arrived(k // PIECES)

    def choose(step, low, high):
        if high - low == 1:
            talk(low)
            return
        mid = (low + high) // 2

        @pl.when(step < mid)
        def _():
            choose(step, low, mid)

        @pl.when(step >= mid)
        def _():
            choose(step, mid, high)

    def turn(step, carry):
        choose(step, 0, STEPS)
        compute(step)
        return carry

    lax.fori_loop(0, STEPS, turn, 0)
    tell(3)

    for count, sem in ((FETCH, yz_send), (OVER, x_send)):
        ref = gath.at[pl.ds(0, len(ARRIVALS) - 1), pl.ds(0, count)]
        pltpu.make_async_copy(ref, ref, sem).wait()
    pltpu.make_async_copy(got, got, a_recv).wait()
    pltpu.make_async_copy(got, got, a_send).wait()
    best = None
    for q in range(4):
        tiles = [got[i - 1] for i in range(q, len(ARRIVALS), 4) if i > 0]
        if q == 0:
            tiles.append(part[0])
        top = functools.reduce(jnp.maximum, tiles)[:, :, q * rows:(q + 1) * rows]
        best = top if best is None else jnp.maximum(best, top)
    nodev[node, :, :, 0:rows] = best
    for j in range(4):
        to = 4 * share + j

        @pl.when(to != node)
        def _():
            pltpu.make_async_remote_copy(
                src_ref=nodev.at[node], dst_ref=nodev.at[node], send_sem=b_send, recv_sem=b_recv,
                device_id=(to, cut), device_id_type=MESH,
            ).start()

    load_trans.wait()
    trans = weights[...]
    mixing = trans / jnp.sum(trans, axis=1, keepdims=True)
    holder = 1 - node // 4
    keeps = holder == core

    @pl.when(keeps)
    def _():
        ref = nodev.at[pl.ds(0, 3)]
        pltpu.make_async_copy(ref, ref, b_recv).wait()
        pltpu.make_async_copy(ref, ref, b_send).wait()

    @pl.when(jnp.logical_not(keeps))
    def _():
        ref = nodev.at[pl.ds(0, 4)]
        pltpu.make_async_copy(ref, ref, b_recv).wait()
        pltpu.make_async_copy(ref, ref, b_send).wait()

    known = jnp.concatenate(
        [nodev[2 * i + holder, m, :, 0:rows] for i in range(NX) for m in range(2)], axis=0
    )
    vals[...] = lax.dot_general(
        known.T, mixing, (((1,), (1,)), ((), ())),
        precision=lax.Precision.HIGHEST, preferred_element_type=jnp.float32,
    )
    out_ref[0] = vals[pl.ds(pl.multiple_of((node % 4) * 8, 8), 8), :]


def per_device(trial_states, cut_slopes, cut_intercepts, transition):
    node_local, cut_local, width = cut_slopes.shape
    rows = trial_states.shape[0]
    nodes = transition.shape[0]
    slope_rows = cut_slopes.reshape(node_local * cut_local, width)
    count = len(ARRIVALS)
    sems = pltpu.SemaphoreType.DMA
    return pl.pallas_call(
        kernel,
        out_shape=jax.ShapeDtypeStruct((1, rows // 8, nodes), jnp.float32),
        in_specs=[pl.BlockSpec(memory_space=pltpu.HBM)] * 4,
        out_specs=pl.BlockSpec(memory_space=pltpu.VMEM),
        scratch_shapes=[
            pltpu.VMEM((count, width // TILE, rows // 2, TILE), jnp.bfloat16),
            pltpu.VMEM((width // TILE, 2 * node_local * cut_local, TILE), jnp.bfloat16),
            pltpu.VMEM((2, node_local, cut_local), jnp.float32),
            pltpu.VMEM(transition.shape, jnp.float32),
            pltpu.VMEM((2, 4 * rows, node_local * cut_local), jnp.float32),
            pltpu.VMEM((count // 4, 2, node_local, 128), jnp.float32),
            pltpu.VMEM((count - 1, 2, node_local, 128), jnp.float32),
            pltpu.VMEM((8, 2, node_local, 128), jnp.float32),
            pltpu.VMEM((rows // 2, nodes), jnp.float32),
            sems((6,)),
            sems((2,)),
            sems((2,)),
            sems(()),
            sems((count - 1, 2)),
            sems(()),
            sems((count // 8,)),
            sems(()),
            sems(()),
            sems(()),
            sems(()),
        ],
        compiler_params=pltpu.CompilerParams(
            collective_id=0, has_side_effects=True, vmem_limit_bytes=40 * 1024 * 1024
        ),
        cost_estimate=pl.CostEstimate(
            flops=2 * 512 * 2048 * 4096, bytes_accessed=5 * 1024 * 1024, transcendentals=0
        ),
    )(*[
        pltpu.with_memory_space_constraint(v, pltpu.HBM)
        for v in (trial_states, slope_rows, cut_intercepts, transition)
    ])


def solution(mesh):
    return jax.shard_map(
        per_device,
        mesh=mesh,
        in_specs=(P("cut", None), P("node", "cut", None), P("node", "cut"), P()),
        out_specs=P("cut", "node", None),
        check_vma=False,
    )
```

```python
import functools

import jax
import jax.numpy as jnp
from jax import lax
from jax.experimental import pallas as pl
from jax.experimental.pallas import tpu as pltpu
from jax.sharding import PartitionSpec as P

MESH = pl.DeviceIdType.MESH

NY, NZ, NX = 4, 8, 4

TILE, OVER, MIDDLE = 128, 10, 12
FETCH = OVER + MIDDLE

PZ, MZ, PY, MY = (0, 1), (0, -1), (1, 0), (-1, 0)
LINKS = (PZ, MZ, PY, MY)

CROSS = {
    PZ: [(0, 1), (0, 2), (0, 3), (2, 1), (0, 4), (2, 2), (2, 3), (1, 4)],
    MZ: [(0, -1), (0, -2), (0, -3), (2, -1), (2, -2), (2, -3), (2, 4)],
    PY: [(1, 0), (2, 0), (1, 1), (1, -1), (1, 2), (1, 3), (1, -2), (1, -3)],
    MY: [(-1, 0), (-1, 1), (-1, -1), (-1, 2), (-1, -2), (-1, 3), (-1, -3), (-1, 4)],
}
PARTS = (0, 1)


def wrap(o):
    return (o[0] % NY, o[1] % NZ)


def plan(window, span, delay):
    todo = {
        d: [(wrap(o), h) for o in order[:-2] for h in PARTS] + [(wrap(o), h) for h in PARTS for o in order[-2:]]
        for d, order in CROSS.items()
    }
    here = {((0, 0), h) for h in PARTS}
    free = dict.fromkeys(LINKS, 0.0)
    flying = dict.fromkeys(LINKS, 0)
    arrivals = []

    def issue(now):
        sends = []
        for d in LINKS:
            for o, h in list(todo[d]):
                source = wrap((o[0] - d[0], o[1] - d[1]))
                if flying[d] < window and (source, h) in here:
                    todo[d].remove((o, h))
                    flying[d] += 1
                    free[d] = max(free[d], now) + span
                    arrivals.append((free[d] + delay, len(arrivals), d, o, h))
                    sends.append((source, h, d))
        return sends

    first = issue(0.0)
    turns = []
    while len(turns) < len(arrivals):
        now, _, d, o, h = sorted(arrivals)[len(turns)]
        here.add((o, h))
        flying[d] -= 1
        turns.append((o, h, issue(now)))
    return first, turns


FIRST, TURNS = plan(window=3, span=1.8, delay=2.5)
DONE = {o: i for i, (o, _, _) in enumerate(TURNS)}
ARRIVALS = [(0, 0)] + sorted(DONE, key=DONE.get)
PLACE = {o: i for i, o in enumerate(ARRIVALS)}
PIECES = 6
STEPS = 4 * PIECES
LAST = 3 * PIECES
NEED = [1 + max(i for i, t in enumerate(TURNS) if PLACE[t[0]] < 8 * g + 8) for g in range(3)]
NEED.append(1 + max(i for i, t in enumerate(TURNS) if t[1] == 0))


def handled(step):
    if step < 0:
        return 0
    group, which = step // PIECES, step % PIECES
    if group < 3:
        return NEED[group] + (NEED[group + 1] - NEED[group]) * which // PIECES
    return NEED[3] + (len(TURNS) - NEED[3]) * min(which, 4) // 4


def kernel(
    trial_ref, slope_ref, offset_ref, trans_ref, out_ref,
    gath, slopes, offset, weights, sums, part, got, nodev, vals,
    local_sem, swap_send, swap_recv, yz_send, yz_recv, x_send, x_recv, a_send, a_recv, b_send, b_recv,
):
    node = lax.axis_index("node")
    cut = lax.axis_index("cut")
    x, core = node // 2, node % 2
    y, z = cut // NZ, cut % NZ
    odd = x % 2
    sibling = x * 2 + 1 - core
    share = 1 - core
    tiles = gath.shape[1]
    own_rows = slope_ref.shape[0]
    rows = gath.shape[2]
    fetch_at = odd * OVER
    mine_at = odd * FETCH
    other_at = (1 - odd) * FETCH
    beside = {d: ((y + d[0] + NY) % NY) * NZ + (z + d[1] + NZ) % NZ for d in LINKS}

    def part_of(o, h):
        return gath.at[PLACE[o], pl.ds(mine_at, OVER) if h == 0 else pl.ds(OVER, MIDDLE)]

    def yz_copy(o, h, d):
        oc = wrap((o[0] + d[0], o[1] + d[1]))
        return pltpu.make_async_remote_copy(
            src_ref=part_of(o, h), dst_ref=part_of(oc, h),
            send_sem=yz_send, recv_sem=yz_recv.at[PLACE[oc] - 1, h],
            device_id=(node, beside[d]), device_id_type=MESH,
        )

    def yz_arrived(o, h):
        ref = part_of(o, h)
        pltpu.make_async_copy(ref, ref, yz_recv.at[PLACE[o] - 1, h]).wait()

    def x_copy(o, way):
        ref = gath.at[PLACE[o], pl.ds(mine_at + way * (OVER // 2), OVER // 2)]
        to = ((x + (1 if way == 0 else NX - 1)) % NX) * 2 + core
        return pltpu.make_async_remote_copy(
            src_ref=ref, dst_ref=ref, send_sem=x_send, recv_sem=x_recv.at[PLACE[o] // 8],
            device_id=(to, cut), device_id_type=MESH,
        )

    def x_arrived(group):
        low = max(8 * group, 1)
        ref = gath.at[pl.ds(low, 8 * group + 8 - low), pl.ds(other_at, OVER)]
        pltpu.make_async_copy(ref, ref, x_recv.at[group]).wait()

    def product(group, at, count, owner):
        low = owner * own_rows
        left = [gath[pl.ds(8 * group, 8), at + k].reshape(8 * rows, TILE) for k in range(count)]
        right = [slopes[at + k, pl.ds(low, own_rows), :] for k in range(count)]
        return lax.dot_general(
            jnp.concatenate(left, axis=1), jnp.concatenate(right, axis=1), (((1,), (1,)), ((), ())),
            preferred_element_type=jnp.float32,
        )

    def maximum(group, owner, rest):
        lane = lax.broadcasted_iota(jnp.int32, (8 * rows, TILE), 1)
        best = jnp.zeros((8 * rows, TILE), jnp.float32)
        for n in range(4):
            at = slice(n * 128, n * 128 + 128)
            total = sums[owner, :, at] + rest[:, at] + offset[owner, n:n + 1, :]
            best = jnp.where(lane == n, jnp.max(total, axis=1, keepdims=True), best)
        turned = best.T
        part[2 * group, owner] = turned[0:4, 0:128]
        part[2 * group + 1, owner] = turned[0:4, 128:256]

    def compute(group, which, ranges):
        owner = lax.rem(core + which, 2)

        @pl.when(which < 2)
        def _():
            sums[owner] = product(group, *ranges[0], owner)

        @pl.when(jnp.logical_and(which >= 2, which < 4))
        def _():
            sums[owner] = sums[owner] + product(group, *ranges[1], owner)

        @pl.when(which >= 4)
        def _():
            maximum(group, owner, product(group, *ranges[2], owner))

    def tell(group):
        for i in range(max(8 * group, 1), 8 * group + 8):
            o = ARRIVALS[i]
            owner = ((y - o[0] + NY) % NY) * NZ + (z - o[1] + NZ) % NZ
            pltpu.make_async_remote_copy(
                src_ref=part.at[i // 4], dst_ref=got.at[i - 1], send_sem=a_send, recv_sem=a_recv,
                device_id=(node, owner), device_id_type=MESH,
            ).start()

    def column(k):
        return pl.ds(pl.multiple_of(k * TILE, TILE), TILE)

    def own(k, sem):
        return pltpu.make_async_copy(
            trial_ref.at[pl.ds(share * rows, rows), column(k)], gath.at[0, k], sem
        )

    own_parts = ((mine_at, OVER, local_sem.at[0]), (OVER, MIDDLE, local_sem.at[4]), (other_at, OVER, local_sem.at[5]))

    def own_arrived(i):
        at, count, sem = own_parts[i]
        ref = gath.at[0, pl.ds(at, count)]
        pltpu.make_async_copy(ref, ref, sem).wait()

    def load(k):
        return pltpu.make_async_copy(
            slope_ref.at[:, column(k)], slopes.at[k, pl.ds(core * own_rows, own_rows)], local_sem.at[1]
        )

    loaded = slopes.at[:, pl.ds(core * own_rows, own_rows)]
    load_offset = pltpu.make_async_copy(offset_ref, offset.at[core], local_sem.at[2])
    load_trans = pltpu.make_async_copy(trans_ref, weights, local_sem.at[3])
    swap = pltpu.make_async_remote_copy(
        src_ref=loaded, dst_ref=loaded, send_sem=swap_send.at[0], recv_sem=swap_recv.at[0],
        device_id=(sibling, cut), device_id_type=MESH,
    )
    swap_offset = pltpu.make_async_remote_copy(
        src_ref=offset_ref, dst_ref=offset.at[core],
        send_sem=swap_send.at[1], recv_sem=swap_recv.at[1],
        device_id=(sibling, cut), device_id_type=MESH,
    )
    barrier = pltpu.get_barrier_semaphore()
    for d in LINKS:
        pl.semaphore_signal(barrier, inc=1, device_id=(node, beside[d]), device_id_type=MESH)
    for j in range(1, 8):
        pl.semaphore_signal(barrier, inc=1, device_id=((node + j) % 8, cut), device_id_type=MESH)
    for at, count, sem in own_parts:
        for k in range(count):
            own(at + k, sem).start()
    load_offset.start()
    load_trans.start()
    pl.semaphore_wait(barrier, 11)
    for part_sent in PARTS:
        own_arrived(part_sent)
        for o, h, d in FIRST:
            if h == part_sent:
                yz_copy(o, h, d).start()
    swap_offset.start()
    for k in range(tiles):
        load(k).start()
    pltpu.make_async_copy(loaded, loaded, local_sem.at[1]).wait()
    swap.start()

    def talk(k):
        for o, h, sends in TURNS[handled(k - 1):handled(k)]:
            yz_arrived(o, h)
            for send in sends:
                yz_copy(*send).start()
            if h == 0:
                x_copy(o, 0).start()
                x_copy(o, 1).start()
        if k == 0:
            own_arrived(2)
            load_offset.wait()
        if k == 1:
            swap_offset.wait()
            swap.wait()
        if k % PIECES == 0 and k > 0:
            tell(k // PIECES - 1)
        if k % PIECES == (2 if k >= LAST else 4):
            x_arrived(k // PIECES)

    def choose(step, low, high):
        if high - low == 1:
            talk(low)
            return
        mid = (low + high) // 2

        @pl.when(step < mid)
        def _():
            choose(step, low, mid)

        @pl.when(step >= mid)
        def _():
            choose(step, mid, high)

    over, middle, other = (mine_at, OVER), (OVER, MIDDLE), (other_at, OVER)

    def turn(step, carry):
        choose(step, 0, LAST)
        compute(lax.div(step, PIECES), lax.rem(step, PIECES), (over, middle, other))
        return carry

    def last_turn(step, carry):
        choose(step, LAST, STEPS)
        compute(3, lax.rem(step, PIECES), (over, other, middle))
        return carry

    lax.fori_loop(0, LAST, turn, 0)
    lax.fori_loop(LAST, STEPS, last_turn, 0)
    tell(3)

    for count, sem in ((FETCH, yz_send), (OVER, x_send)):
        ref = gath.at[pl.ds(0, len(ARRIVALS) - 1), pl.ds(0, count)]
        pltpu.make_async_copy(ref, ref, sem).wait()
    pltpu.make_async_copy(got, got, a_recv).wait()
    pltpu.make_async_copy(got, got, a_send).wait()
    best = None
    for q in range(4):
        tiles = [got[i - 1] for i in range(q, len(ARRIVALS), 4) if i > 0]
        if q == 0:
            tiles.append(part[0])
        top = functools.reduce(jnp.maximum, tiles)[:, :, q * rows:(q + 1) * rows]
        best = top if best is None else jnp.maximum(best, top)
    nodev[node, :, :, 0:rows] = best
    for j in range(4):
        to = 4 * share + j

        @pl.when(to != node)
        def _():
            pltpu.make_async_remote_copy(
                src_ref=nodev.at[node], dst_ref=nodev.at[node], send_sem=b_send, recv_sem=b_recv,
                device_id=(to, cut), device_id_type=MESH,
            ).start()

    load_trans.wait()
    trans = weights[...]
    mixing = trans / jnp.sum(trans, axis=1, keepdims=True)
    holder = 1 - node // 4
    keeps = holder == core

    @pl.when(keeps)
    def _():
        ref = nodev.at[pl.ds(0, 3)]
        pltpu.make_async_copy(ref, ref, b_recv).wait()
        pltpu.make_async_copy(ref, ref, b_send).wait()

    @pl.when(jnp.logical_not(keeps))
    def _():
        ref = nodev.at[pl.ds(0, 4)]
        pltpu.make_async_copy(ref, ref, b_recv).wait()
        pltpu.make_async_copy(ref, ref, b_send).wait()

    known = jnp.concatenate(
        [nodev[2 * i + holder, m, :, 0:rows] for i in range(NX) for m in range(2)], axis=0
    )
    vals[...] = lax.dot_general(
        known.T, mixing, (((1,), (1,)), ((), ())),
        precision=lax.Precision.HIGHEST, preferred_element_type=jnp.float32,
    )
    out_ref[0] = vals[pl.ds(pl.multiple_of((node % 4) * 8, 8), 8), :]


def per_device(trial_states, cut_slopes, cut_intercepts, transition):
    node_local, cut_local, width = cut_slopes.shape
    rows = trial_states.shape[0]
    nodes = transition.shape[0]
    slope_rows = cut_slopes.reshape(node_local * cut_local, width)
    count = len(ARRIVALS)
    sems = pltpu.SemaphoreType.DMA
    return pl.pallas_call(
        kernel,
        out_shape=jax.ShapeDtypeStruct((1, rows // 8, nodes), jnp.float32),
        in_specs=[pl.BlockSpec(memory_space=pltpu.HBM)] * 4,
        out_specs=pl.BlockSpec(memory_space=pltpu.VMEM),
        scratch_shapes=[
            pltpu.VMEM((count, width // TILE, rows // 2, TILE), jnp.bfloat16),
            pltpu.VMEM((width // TILE, 2 * node_local * cut_local, TILE), jnp.bfloat16),
            pltpu.VMEM((2, node_local, cut_local), jnp.float32),
            pltpu.VMEM(transition.shape, jnp.float32),
            pltpu.VMEM((2, 4 * rows, node_local * cut_local), jnp.float32),
            pltpu.VMEM((count // 4, 2, node_local, 128), jnp.float32),
            pltpu.VMEM((count - 1, 2, node_local, 128), jnp.float32),
            pltpu.VMEM((8, 2, node_local, 128), jnp.float32),
            pltpu.VMEM((rows // 2, nodes), jnp.float32),
            sems((6,)),
            sems((2,)),
            sems((2,)),
            sems(()),
            sems((count - 1, 2)),
            sems(()),
            sems((count // 8,)),
            sems(()),
            sems(()),
            sems(()),
            sems(()),
        ],
        compiler_params=pltpu.CompilerParams(
            collective_id=0, has_side_effects=True, vmem_limit_bytes=40 * 1024 * 1024
        ),
        cost_estimate=pl.CostEstimate(
            flops=2 * 512 * 2048 * 4096, bytes_accessed=5 * 1024 * 1024, transcendentals=0
        ),
    )(*[
        pltpu.with_memory_space_constraint(v, pltpu.HBM)
        for v in (trial_states, slope_rows, cut_intercepts, transition)
    ])


def solution(mesh):
    return jax.shard_map(
        per_device,
        mesh=mesh,
        in_specs=(P("cut", None), P("node", "cut", None), P("node", "cut"), P()),
        out_specs=P("cut", "node", None),
        check_vma=False,
    )
```

```python
import functools

import jax
import jax.numpy as jnp
from jax import lax
from jax.experimental import pallas as pl
from jax.experimental.pallas import tpu as pltpu
from jax.sharding import PartitionSpec as P

MESH = pl.DeviceIdType.MESH

NY, NZ, NX = 4, 8, 4

TILE, OVER, MIDDLE = 128, 10, 12
FETCH = OVER + MIDDLE

PZ, MZ, PY, MY = (0, 1), (0, -1), (1, 0), (-1, 0)
LINKS = (PZ, MZ, PY, MY)

CROSS = {
    PZ: [(0, 1), (0, 2), (0, 3), (2, 1), (0, 4), (2, 2), (2, 3), (1, 4)],
    MZ: [(0, -1), (0, -2), (0, -3), (2, -1), (2, -2), (2, -3), (2, 4)],
    PY: [(1, 0), (2, 0), (1, 1), (1, -1), (1, 2), (1, -2), (1, 3), (1, -3)],
    MY: [(-1, 0), (-1, 1), (-1, -1), (-1, 2), (-1, -2), (-1, 3), (-1, -3), (-1, 4)],
}
PARTS = (0, 1)


def wrap(o):
    return (o[0] % NY, o[1] % NZ)


def plan(window, span, delay):
    todo = {d: [(wrap(o), h) for o in order for h in PARTS] for d, order in CROSS.items()}
    here = {((0, 0), h) for h in PARTS}
    free = dict.fromkeys(LINKS, 0.0)
    flying = dict.fromkeys(LINKS, 0)
    arrivals = []

    def issue(now):
        sends = []
        for d in LINKS:
            for o, h in list(todo[d]):
                source = wrap((o[0] - d[0], o[1] - d[1]))
                if flying[d] < window and (source, h) in here:
                    todo[d].remove((o, h))
                    flying[d] += 1
                    free[d] = max(free[d], now) + span
                    arrivals.append((free[d] + delay, len(arrivals), d, o, h))
                    sends.append((source, h, d))
        return sends

    first = issue(0.0)
    turns = []
    while len(turns) < len(arrivals):
        now, _, d, o, h = sorted(arrivals)[len(turns)]
        here.add((o, h))
        flying[d] -= 1
        turns.append((o, h, issue(now)))
    return first, turns


FIRST, TURNS = plan(window=3, span=1.8, delay=2.5)
PLACE = {(0, 0): 0}
for o, h, _ in TURNS:
    if (o, 1 - h) in [t[:2] for t in TURNS[:TURNS.index((o, h, _))]]:
        PLACE[o] = len(PLACE)
ARRIVALS = sorted(PLACE, key=PLACE.get)
GROUPS = ((0, 4), (4, 4), (8, 8), (16, 8), (24, 8))
GROUP_OF = {first + i: g for g, (first, size) in enumerate(GROUPS) for i in range(size)}
NEED = [1 + max(i for i, t in enumerate(TURNS) if PLACE[t[0]] < first + size) for first, size in GROUPS]
SMALL, BOTH, LARGE, STEPS = 0, 4, 6, 18
KNOTS = ((0, NEED[0]), (2, NEED[1]), (6, NEED[2]), (10, NEED[3]), (14, NEED[4]), (STEPS, NEED[4]))
CROSSED = {1: 0, 3: 1, 8: 2, 12: 3, 16: 4}
TOLD = {6: (0, 8), 10: (8, 8), 14: (16, 8)}


def handled(step):
    if step < 0:
        return 0
    low, high = [(p, q) for p, q in zip(KNOTS, KNOTS[1:]) if p[0] <= step < q[0]][0]
    return low[1] + (high[1] - low[1]) * (step - low[0]) // (high[0] - low[0])


def kernel(
    trial_ref, slope_ref, offset_ref, trans_ref, out_ref,
    gath, slopes, offset, weights, mixing, sums, part, got, give, take,
    local_sem, swap_send, swap_recv, yz_send, yz_recv, x_send, x_recv, a_send, a_recv, b_send, b_recv,
):
    node = lax.axis_index("node")
    cut = lax.axis_index("cut")
    x, core = node // 2, node % 2
    y, z = cut // NZ, cut % NZ
    odd = x % 2
    sibling = x * 2 + 1 - core
    share = 1 - core
    tiles = gath.shape[1]
    own_rows = slope_ref.shape[0]
    rows = gath.shape[2]
    fetch_at = odd * OVER
    mine_at = odd * FETCH
    other_at = (1 - odd) * FETCH
    beside = {d: ((y + d[0] + NY) % NY) * NZ + (z + d[1] + NZ) % NZ for d in LINKS}

    def part_of(o, h):
        return gath.at[PLACE[o], pl.ds(mine_at, OVER) if h == 0 else pl.ds(OVER, MIDDLE)]

    def yz_copy(o, h, d):
        oc = wrap((o[0] + d[0], o[1] + d[1]))
        return pltpu.make_async_remote_copy(
            src_ref=part_of(o, h), dst_ref=part_of(oc, h),
            send_sem=yz_send, recv_sem=yz_recv.at[PLACE[oc] - 1, h],
            device_id=(node, beside[d]), device_id_type=MESH,
        )

    def yz_arrived(o, h):
        ref = part_of(o, h)
        pltpu.make_async_copy(ref, ref, yz_recv.at[PLACE[o] - 1, h]).wait()

    def x_copy(o, way):
        ref = gath.at[PLACE[o], pl.ds(mine_at + way * (OVER // 2), OVER // 2)]
        to = ((x + (1 if way == 0 else NX - 1)) % NX) * 2 + core
        return pltpu.make_async_remote_copy(
            src_ref=ref, dst_ref=ref, send_sem=x_send, recv_sem=x_recv.at[GROUP_OF[PLACE[o]]],
            device_id=(to, cut), device_id_type=MESH,
        )

    def x_arrived(group):
        first, size = GROUPS[group]
        low = max(first, 1)
        ref = gath.at[pl.ds(low, first + size - low), pl.ds(other_at, OVER)]
        pltpu.make_async_copy(ref, ref, x_recv.at[group]).wait()

    def product(first, size, at, count, owner):
        low = owner * own_rows
        left = [gath[pl.ds(first, size), at + k].reshape(size * rows, TILE) for k in range(count)]
        right = [slopes[at + k, pl.ds(low, own_rows), :] for k in range(count)]
        return lax.dot_general(
            jnp.concatenate(left, axis=1), jnp.concatenate(right, axis=1), (((1,), (1,)), ((), ())),
            preferred_element_type=jnp.float32,
        )

    def compute(first, size, which):
        owner = lax.rem(core + which, 2)
        count = size * rows

        @pl.when(which < 2)
        def _():
            sums[owner, 0:count] = product(first, size, fetch_at, FETCH, owner)

        @pl.when(which >= 2)
        def _():
            rest = product(first, size, other_at, OVER, owner)
            lane = lax.broadcasted_iota(jnp.int32, (count, TILE), 1)
            best = jnp.zeros((count, TILE), jnp.float32)
            for n in range(4):
                at = slice(n * 128, n * 128 + 128)
                total = sums[owner, 0:count, at] + rest[:, at] + offset[owner, n:n + 1, :]
                best = jnp.where(lane == n, jnp.max(total, axis=1, keepdims=True), best)
            turned = best.T
            for j in range(size // 4):
                part[first // 4 + j, owner] = turned[0:4, 128 * j:128 * j + 128]

    def tell(first, size):
        for i in range(max(first, 1), first + size):
            o = ARRIVALS[i]
            owner = ((y - o[0] + NY) % NY) * NZ + (z - o[1] + NZ) % NZ
            pltpu.make_async_remote_copy(
                src_ref=part.at[i // 4], dst_ref=got.at[i - 1], send_sem=a_send, recv_sem=a_recv,
                device_id=(node, owner), device_id_type=MESH,
            ).start()

    def column(k):
        return pl.ds(pl.multiple_of(k * TILE, TILE), TILE)

    def own(k, sem):
        return pltpu.make_async_copy(
            trial_ref.at[pl.ds(share * rows, rows), column(k)], gath.at[0, k], sem
        )

    own_parts = ((mine_at, OVER, local_sem.at[0]), (OVER, MIDDLE, local_sem.at[4]), (other_at, OVER, local_sem.at[5]))

    def own_arrived(i):
        at, count, sem = own_parts[i]
        ref = gath.at[0, pl.ds(at, count)]
        pltpu.make_async_copy(ref, ref, sem).wait()

    def load(k):
        return pltpu.make_async_copy(
            slope_ref.at[:, column(k)], slopes.at[k, pl.ds(core * own_rows, own_rows)], local_sem.at[1]
        )

    loaded = slopes.at[:, pl.ds(core * own_rows, own_rows)]
    load_offset = pltpu.make_async_copy(offset_ref, offset.at[core], local_sem.at[2])
    load_trans = pltpu.make_async_copy(trans_ref, weights, local_sem.at[3])
    swap = pltpu.make_async_remote_copy(
        src_ref=loaded, dst_ref=loaded, send_sem=swap_send.at[0], recv_sem=swap_recv.at[0],
        device_id=(sibling, cut), device_id_type=MESH,
    )
    swap_offset = pltpu.make_async_remote_copy(
        src_ref=offset_ref, dst_ref=offset.at[core],
        send_sem=swap_send.at[1], recv_sem=swap_recv.at[1],
        device_id=(sibling, cut), device_id_type=MESH,
    )
    barrier = pltpu.get_barrier_semaphore()
    for d in LINKS:
        pl.semaphore_signal(barrier, inc=1, device_id=(node, beside[d]), device_id_type=MESH)
    for j in range(1, 8):
        pl.semaphore_signal(barrier, inc=1, device_id=((node + j) % 8, cut), device_id_type=MESH)
    for at, count, sem in own_parts:
        for k in range(count):
            own(at + k, sem).start()
    load_offset.start()
    load_trans.start()
    pl.semaphore_wait(barrier, 11)
    for part_sent in PARTS:
        own_arrived(part_sent)
        for o, h, d in FIRST:
            if h == part_sent:
                yz_copy(o, h, d).start()
    swap_offset.start()
    for k in range(tiles):
        load(k).start()
    pltpu.make_async_copy(loaded, loaded, local_sem.at[1]).wait()
    swap.start()
    load_trans.wait()
    trans = weights[...]
    mixing[...] = (trans / jnp.sum(trans, axis=1, keepdims=True)).T

    def talk(k):
        for o, h, sends in TURNS[handled(k - 1):handled(k)]:
            yz_arrived(o, h)
            for send in sends:
                yz_copy(*send).start()
            if h == 0:
                x_copy(o, 0).start()
                x_copy(o, 1).start()
        if k == 0:
            own_arrived(2)
            load_offset.wait()
        if k == BOTH:
            swap_offset.wait()
            swap.wait()
        if k in TOLD:
            tell(*TOLD[k])
        if k in CROSSED:
            x_arrived(CROSSED[k])

    def choose(step, low, high):
        if high - low == 1:
            talk(low)
            return
        mid = (low + high) // 2

        @pl.when(step < mid)
        def _():
            choose(step, low, mid)

        @pl.when(step >= mid)
        def _():
            choose(step, mid, high)

    def small_turn(step, carry):
        choose(step, SMALL, BOTH)
        compute(4 * lax.div(step, 2), 4, 2 * lax.rem(step, 2))
        return carry

    def turn(step, carry):
        choose(step, BOTH, STEPS)
        both = step < LARGE
        first = jnp.where(both, 0, 8 + 8 * lax.div(step - LARGE, 4))
        compute(first, 8, jnp.where(both, 2 * (step - BOTH) + 1, lax.rem(step - LARGE, 4)))
        return carry

    lax.fori_loop(SMALL, BOTH, small_turn, 0)
    lax.fori_loop(BOTH, STEPS, turn, 0)
    tell(24, 8)

    for count, sem in ((FETCH, yz_send), (OVER, x_send)):
        ref = gath.at[pl.ds(0, len(ARRIVALS) - 1), pl.ds(0, count)]
        pltpu.make_async_copy(ref, ref, sem).wait()
    pltpu.make_async_copy(got, got, a_recv).wait()
    pltpu.make_async_copy(got, got, a_send).wait()
    best = None
    for q in range(4):
        tiles = [got[i - 1] for i in range(q, len(ARRIVALS), 4) if i > 0]
        if q == 0:
            tiles.append(part[0])
        top = functools.reduce(jnp.maximum, tiles)[:, :, q * rows:(q + 1) * rows]
        best = top if best is None else jnp.maximum(best, top)
    states_down = jnp.concatenate([best[0], best[1]], axis=0).T
    shares = mixing[pl.ds(pl.multiple_of(x * 8, 8), 8), :]
    values = sum(states_down[:, i:i + 1] * shares[i:i + 1, :] for i in range(8))
    for j in range(4):
        give[j, :, 0:shares.shape[1]] = values[8 * j:8 * j + 8]
    for j in range(4):
        to = 4 * share + j

        @pl.when(to != node)
        def _():
            pltpu.make_async_remote_copy(
                src_ref=give.at[j], dst_ref=take.at[x], send_sem=b_send, recv_sem=b_recv,
                device_id=(to, cut), device_id_type=MESH,
            ).start()

        @pl.when(to == node)
        def _():
            take[x] = give[j]

    keeps = 1 - node // 4 == core

    @pl.when(keeps)
    def _():
        ref = take.at[pl.ds(0, 3)]
        pltpu.make_async_copy(ref, ref, b_recv).wait()
        pltpu.make_async_copy(ref, ref, b_send).wait()

    @pl.when(jnp.logical_not(keeps))
    def _():
        pltpu.make_async_copy(take, take, b_recv).wait()
        pltpu.make_async_copy(take, take, b_send).wait()

    out_ref[0] = sum(take[i, :, 0:shares.shape[1]] for i in range(NX))


def per_device(trial_states, cut_slopes, cut_intercepts, transition):
    node_local, cut_local, width = cut_slopes.shape
    rows = trial_states.shape[0]
    nodes = transition.shape[0]
    slope_rows = cut_slopes.reshape(node_local * cut_local, width)
    count = len(ARRIVALS)
    sems = pltpu.SemaphoreType.DMA
    return pl.pallas_call(
        kernel,
        out_shape=jax.ShapeDtypeStruct((1, rows // 8, nodes), jnp.float32),
        in_specs=[pl.BlockSpec(memory_space=pltpu.HBM)] * 4,
        out_specs=pl.BlockSpec(memory_space=pltpu.VMEM),
        scratch_shapes=[
            pltpu.VMEM((count, width // TILE, rows // 2, TILE), jnp.bfloat16),
            pltpu.VMEM((width // TILE, 2 * node_local * cut_local, TILE), jnp.bfloat16),
            pltpu.VMEM((2, node_local, cut_local), jnp.float32),
            pltpu.VMEM(transition.shape, jnp.float32),
            pltpu.VMEM(transition.shape, jnp.float32),
            pltpu.VMEM((2, 4 * rows, node_local * cut_local), jnp.float32),
            pltpu.VMEM((count // 4, 2, node_local, 128), jnp.float32),
            pltpu.VMEM((count - 1, 2, node_local, 128), jnp.float32),
            pltpu.VMEM((4, 8, 128), jnp.float32),
            pltpu.VMEM((4, 8, 128), jnp.float32),
            sems((6,)),
            sems((2,)),
            sems((2,)),
            sems(()),
            sems((count - 1, 2)),
            sems(()),
            sems((len(GROUPS),)),
            sems(()),
            sems(()),
            sems(()),
            sems(()),
        ],
        compiler_params=pltpu.CompilerParams(
            collective_id=0, has_side_effects=True, vmem_limit_bytes=40 * 1024 * 1024
        ),
        cost_estimate=pl.CostEstimate(
            flops=2 * 512 * 2048 * 4096, bytes_accessed=5 * 1024 * 1024, transcendentals=0
        ),
    )(*[
        pltpu.with_memory_space_constraint(v, pltpu.HBM)
        for v in (trial_states, slope_rows, cut_intercepts, transition)
    ])


def solution(mesh):
    return jax.shard_map(
        per_device,
        mesh=mesh,
        in_specs=(P("cut", None), P("node", "cut", None), P("node", "cut"), P()),
        out_specs=P("cut", "node", None),
        check_vma=False,
    )
```

```python
import functools

import jax
import jax.numpy as jnp
from jax import lax
from jax.experimental import pallas as pl
from jax.experimental.pallas import tpu as pltpu
from jax.sharding import PartitionSpec as P

MESH = pl.DeviceIdType.MESH

NY, NZ, NX = 4, 8, 4

TILE, OVER, MIDDLE = 128, 10, 12
FETCH = OVER + MIDDLE

PZ, MZ, PY, MY = (0, 1), (0, -1), (1, 0), (-1, 0)
LINKS = (PZ, MZ, PY, MY)

CROSS = {
    PZ: [(0, 1), (0, 2), (0, 3), (2, 1), (0, 4), (2, 2), (2, 3), (1, 4)],
    MZ: [(0, -1), (0, -2), (0, -3), (2, -1), (2, -2), (2, -3), (2, 4)],
    PY: [(1, 0), (2, 0), (1, 1), (1, -1), (1, 2), (1, -2), (1, 3), (1, -3)],
    MY: [(-1, 0), (-1, 1), (-1, -1), (-1, 2), (-1, -2), (-1, 3), (-1, -3), (-1, 4)],
}
PARTS = (0, 1, 2, 3)
OVER_PARTS = (0, 1)
SPANS = ((0, 5), (5, 5), (OVER, 6), (OVER + 6, 6))
TREES = (((1, 1), False), ((1, -1), False), ((1, 1), True), ((-1, 1), True))


def wrap(o):
    return (o[0] % NY, o[1] % NZ)


def arrival_links():
    links = {}
    for p, ((sy, sz), moved) in enumerate(TREES):
        for d, order in CROSS.items():
            for turn, o in enumerate(order):
                d_here, turn_here = d, turn
                if moved and o == (-1, 4):
                    d_here, turn_here = MZ, len(order)
                links[wrap((sy * o[0], sz * o[1])), p] = (sy * d_here[0], sz * d_here[1]), turn_here
    return links


def plan(window, span, delay):
    links = arrival_links()
    todo = {d: sorted((k for k in links if links[k][0] == d), key=lambda k: (links[k][1], k[1])) for d in LINKS}
    here = {((0, 0), h) for h in PARTS}
    free = dict.fromkeys(LINKS, 0.0)
    flying = dict.fromkeys(LINKS, 0)
    arrivals = []

    def issue(now):
        sends = []
        for d in LINKS:
            for o, h in list(todo[d]):
                source = wrap((o[0] - d[0], o[1] - d[1]))
                if flying[d] < window and (source, h) in here:
                    todo[d].remove((o, h))
                    flying[d] += 1
                    free[d] = max(free[d], now) + span
                    arrivals.append((free[d] + delay, len(arrivals), d, o, h))
                    sends.append((source, h, d))
        return sends

    first = issue(0.0)
    turns = []
    while len(turns) < len(arrivals):
        now, _, d, o, h = sorted(arrivals)[len(turns)]
        here.add((o, h))
        flying[d] -= 1
        turns.append((o, h, issue(now)))
    return first, turns


FIRST, TURNS = plan(window=6, span=1.1, delay=2.0)
DONE = {o: i for i, (o, _, _) in enumerate(TURNS)}
ARRIVALS = [(0, 0)] + sorted(DONE, key=DONE.get)
PLACE = {o: i for i, o in enumerate(ARRIVALS)}
PIECES = 4
NEED = [1 + max(i for i, t in enumerate(TURNS) if PLACE[t[0]] < 8 * g + 8) for g in range(4)]
STEPS = 4 * PIECES


def handled(step):
    group, which = step // PIECES, step % PIECES
    if step < 0:
        return 0
    return NEED[group] + (NEED[min(group + 1, 3)] - NEED[group]) * which // PIECES


def kernel(
    trial_ref, slope_ref, offset_ref, trans_ref, out_ref,
    gath, slopes, offset, weights, sums, part, got, nodev, vals,
    local_sem, swap_send, swap_recv, yz_send, yz_recv, x_send, x_recv, a_send, a_recv, b_send, b_recv,
):
    node = lax.axis_index("node")
    cut = lax.axis_index("cut")
    x, core = node // 2, node % 2
    y, z = cut // NZ, cut % NZ
    odd = x % 2
    sibling = x * 2 + 1 - core
    share = 1 - core
    tiles = gath.shape[1]
    own_rows = slope_ref.shape[0]
    rows = gath.shape[2]
    fetch_at = odd * OVER
    mine_at = odd * FETCH
    other_at = (1 - odd) * FETCH
    beside = {d: ((y + d[0] + NY) % NY) * NZ + (z + d[1] + NZ) % NZ for d in LINKS}

    def part_of(o, h):
        at, count = SPANS[h]
        return gath.at[PLACE[o], pl.ds(at + mine_at if h in OVER_PARTS else at, count)]

    def yz_copy(o, h, d):
        oc = wrap((o[0] + d[0], o[1] + d[1]))
        return pltpu.make_async_remote_copy(
            src_ref=part_of(o, h), dst_ref=part_of(oc, h),
            send_sem=yz_send, recv_sem=yz_recv.at[PLACE[oc] - 1, h],
            device_id=(node, beside[d]), device_id_type=MESH,
        )

    def yz_arrived(o, h):
        ref = part_of(o, h)
        pltpu.make_async_copy(ref, ref, yz_recv.at[PLACE[o] - 1, h]).wait()

    def x_copy(o, h):
        ref = part_of(o, h)
        to = ((x + (1 if (PLACE[o] + h) % 2 else NX - 1)) % NX) * 2 + core
        return pltpu.make_async_remote_copy(
            src_ref=ref, dst_ref=ref, send_sem=x_send, recv_sem=x_recv.at[PLACE[o] // 8],
            device_id=(to, cut), device_id_type=MESH,
        )

    def x_arrived(group):
        low = max(8 * group, 1)
        ref = gath.at[pl.ds(low, 8 * group + 8 - low), pl.ds(other_at, OVER)]
        pltpu.make_async_copy(ref, ref, x_recv.at[group]).wait()

    def product(group, at, count, owner):
        low = owner * own_rows
        left = [gath[pl.ds(8 * group, 8), at + k].reshape(8 * rows, TILE) for k in range(count)]
        right = [slopes[at + k, pl.ds(low, own_rows), :] for k in range(count)]
        return lax.dot_general(
            jnp.concatenate(left, axis=1), jnp.concatenate(right, axis=1), (((1,), (1,)), ((), ())),
            preferred_element_type=jnp.float32,
        )

    def compute(piece):
        group = lax.div(piece, PIECES)
        which = lax.rem(piece, PIECES)
        owner = lax.rem(core + which, 2)

        @pl.when(which < 2)
        def _():
            sums[owner] = product(group, fetch_at, FETCH, owner)

        @pl.when(which >= 2)
        def _():
            rest = product(group, other_at, OVER, owner)
            lane = lax.broadcasted_iota(jnp.int32, (8 * rows, TILE), 1)
            best = jnp.zeros((8 * rows, TILE), jnp.float32)
            for n in range(4):
                at = slice(n * 128, n * 128 + 128)
                total = sums[owner, :, at] + rest[:, at] + offset[owner, n:n + 1, :]
                best = jnp.where(lane == n, jnp.max(total, axis=1, keepdims=True), best)
            turned = best.T
            part[2 * group, owner] = turned[0:4, 0:128]
            part[2 * group + 1, owner] = turned[0:4, 128:256]

    def tell(group):
        for i in range(max(8 * group, 1), 8 * group + 8):
            o = ARRIVALS[i]
            owner = ((y - o[0] + NY) % NY) * NZ + (z - o[1] + NZ) % NZ
            pltpu.make_async_remote_copy(
                src_ref=part.at[i // 4], dst_ref=got.at[i - 1], send_sem=a_send, recv_sem=a_recv,
                device_id=(node, owner), device_id_type=MESH,
            ).start()

    def column(k):
        return pl.ds(pl.multiple_of(k * TILE, TILE), TILE)

    def own(k, sem):
        return pltpu.make_async_copy(
            trial_ref.at[pl.ds(share * rows, rows), column(k)], gath.at[0, k], sem
        )

    own_parts = ((mine_at, OVER, local_sem.at[0]), (OVER, MIDDLE, local_sem.at[4]), (other_at, OVER, local_sem.at[5]))

    def own_arrived(i):
        at, count, sem = own_parts[i]
        ref = gath.at[0, pl.ds(at, count)]
        pltpu.make_async_copy(ref, ref, sem).wait()

    def load(k):
        return pltpu.make_async_copy(
            slope_ref.at[:, column(k)], slopes.at[k, pl.ds(core * own_rows, own_rows)], local_sem.at[1]
        )

    loaded = slopes.at[:, pl.ds(core * own_rows, own_rows)]
    load_offset = pltpu.make_async_copy(offset_ref, offset.at[core], local_sem.at[2])
    load_trans = pltpu.make_async_copy(trans_ref, weights, local_sem.at[3])
    swap = pltpu.make_async_remote_copy(
        src_ref=loaded, dst_ref=loaded, send_sem=swap_send.at[0], recv_sem=swap_recv.at[0],
        device_id=(sibling, cut), device_id_type=MESH,
    )
    swap_offset = pltpu.make_async_remote_copy(
        src_ref=offset_ref, dst_ref=offset.at[core],
        send_sem=swap_send.at[1], recv_sem=swap_recv.at[1],
        device_id=(sibling, cut), device_id_type=MESH,
    )
    barrier = pltpu.get_barrier_semaphore()
    for d in LINKS:
        pl.semaphore_signal(barrier, inc=1, device_id=(node, beside[d]), device_id_type=MESH)
    for j in range(1, 8):
        pl.semaphore_signal(barrier, inc=1, device_id=((node + j) % 8, cut), device_id_type=MESH)
    for at, count, sem in own_parts:
        for k in range(count):
            own(at + k, sem).start()
    load_offset.start()
    load_trans.start()
    pl.semaphore_wait(barrier, 11)
    own_arrived(0)
    for o, h, d in FIRST:
        if h in OVER_PARTS:
            yz_copy(o, h, d).start()
    own_arrived(1)
    for o, h, d in FIRST:
        if h not in OVER_PARTS:
            yz_copy(o, h, d).start()
    swap_offset.start()
    for k in range(tiles):
        load(k).start()
    pltpu.make_async_copy(loaded, loaded, local_sem.at[1]).wait()
    swap.start()

    def talk(k):
        for o, h, sends in TURNS[handled(k - 1):handled(k)]:
            yz_arrived(o, h)
            for send in sends:
                yz_copy(*send).start()
            if h in OVER_PARTS:
                x_copy(o, h).start()
        if k == 0:
            own_arrived(2)
            load_offset.wait()
        if k == 1:
            swap_offset.wait()
            swap.wait()
        if k % PIECES == 0 and k > 0:
            tell(k // PIECES - 1)
        if k % PIECES == PIECES // 2:
            x_arrived(k // PIECES)

    def choose(step, low, high):
        if high - low == 1:
            talk(low)
            return
        mid = (low + high) // 2

        @pl.when(step < mid)
        def _():
            choose(step, low, mid)

        @pl.when(step >= mid)
        def _():
            choose(step, mid, high)

    def turn(step, carry):
        choose(step, 0, STEPS)
        compute(step)
        return carry

    lax.fori_loop(0, STEPS, turn, 0)
    tell(3)

    for count, sem in ((FETCH, yz_send), (OVER, x_send)):
        ref = gath.at[pl.ds(0, len(ARRIVALS) - 1), pl.ds(0, count)]
        pltpu.make_async_copy(ref, ref, sem).wait()
    pltpu.make_async_copy(got, got, a_recv).wait()
    pltpu.make_async_copy(got, got, a_send).wait()
    best = None
    for q in range(4):
        tiles = [got[i - 1] for i in range(q, len(ARRIVALS), 4) if i > 0]
        if q == 0:
            tiles.append(part[0])
        top = functools.reduce(jnp.maximum, tiles)[:, :, q * rows:(q + 1) * rows]
        best = top if best is None else jnp.maximum(best, top)
    nodev[node, :, :, 0:rows] = best
    for j in range(4):
        to = 4 * share + j

        @pl.when(to != node)
        def _():
            pltpu.make_async_remote_copy(
                src_ref=nodev.at[node], dst_ref=nodev.at[node], send_sem=b_send, recv_sem=b_recv,
                device_id=(to, cut), device_id_type=MESH,
            ).start()

    load_trans.wait()
    trans = weights[...]
    mixing = trans / jnp.sum(trans, axis=1, keepdims=True)
    holder = 1 - node // 4
    keeps = holder == core

    @pl.when(keeps)
    def _():
        ref = nodev.at[pl.ds(0, 3)]
        pltpu.make_async_copy(ref, ref, b_recv).wait()
        pltpu.make_async_copy(ref, ref, b_send).wait()

    @pl.when(jnp.logical_not(keeps))
    def _():
        ref = nodev.at[pl.ds(0, 4)]
        pltpu.make_async_copy(ref, ref, b_recv).wait()
        pltpu.make_async_copy(ref, ref, b_send).wait()

    known = jnp.concatenate(
        [nodev[2 * i + holder, m, :, 0:rows] for i in range(NX) for m in range(2)], axis=0
    )
    vals[...] = lax.dot_general(
        known.T, mixing, (((1,), (1,)), ((), ())),
        precision=lax.Precision.HIGHEST, preferred_element_type=jnp.float32,
    )
    out_ref[0] = vals[pl.ds(pl.multiple_of((node % 4) * 8, 8), 8), :]


def per_device(trial_states, cut_slopes, cut_intercepts, transition):
    node_local, cut_local, width = cut_slopes.shape
    rows = trial_states.shape[0]
    nodes = transition.shape[0]
    slope_rows = cut_slopes.reshape(node_local * cut_local, width)
    count = len(ARRIVALS)
    sems = pltpu.SemaphoreType.DMA
    return pl.pallas_call(
        kernel,
        out_shape=jax.ShapeDtypeStruct((1, rows // 8, nodes), jnp.float32),
        in_specs=[pl.BlockSpec(memory_space=pltpu.HBM)] * 4,
        out_specs=pl.BlockSpec(memory_space=pltpu.VMEM),
        scratch_shapes=[
            pltpu.VMEM((count, width // TILE, rows // 2, TILE), jnp.bfloat16),
            pltpu.VMEM((width // TILE, 2 * node_local * cut_local, TILE), jnp.bfloat16),
            pltpu.VMEM((2, node_local, cut_local), jnp.float32),
            pltpu.VMEM(transition.shape, jnp.float32),
            pltpu.VMEM((2, 4 * rows, node_local * cut_local), jnp.float32),
            pltpu.VMEM((count // 4, 2, node_local, 128), jnp.float32),
            pltpu.VMEM((count - 1, 2, node_local, 128), jnp.float32),
            pltpu.VMEM((8, 2, node_local, 128), jnp.float32),
            pltpu.VMEM((rows // 2, nodes), jnp.float32),
            sems((6,)),
            sems((2,)),
            sems((2,)),
            sems(()),
            sems((count - 1, len(PARTS))),
            sems(()),
            sems((count // 8,)),
            sems(()),
            sems(()),
            sems(()),
            sems(()),
        ],
        compiler_params=pltpu.CompilerParams(
            collective_id=0, has_side_effects=True, vmem_limit_bytes=40 * 1024 * 1024
        ),
        cost_estimate=pl.CostEstimate(
            flops=2 * 512 * 2048 * 4096, bytes_accessed=5 * 1024 * 1024, transcendentals=0
        ),
    )(*[
        pltpu.with_memory_space_constraint(v, pltpu.HBM)
        for v in (trial_states, slope_rows, cut_intercepts, transition)
    ])


def solution(mesh):
    return jax.shard_map(
        per_device,
        mesh=mesh,
        in_specs=(P("cut", None), P("node", "cut", None), P("node", "cut"), P()),
        out_specs=P("cut", "node", None),
        check_vma=False,
    )
```

```python
import functools

import jax
import jax.numpy as jnp
from jax import lax
from jax.experimental import pallas as pl
from jax.experimental.pallas import tpu as pltpu
from jax.sharding import PartitionSpec as P

MESH = pl.DeviceIdType.MESH

NY, NZ, NX = 4, 8, 4

TILE, OVER, MIDDLE = 128, 11, 10
FETCH = OVER + MIDDLE

PZ, MZ, PY, MY = (0, 1), (0, -1), (1, 0), (-1, 0)
LINKS = (PZ, MZ, PY, MY)

CROSS = {
    PZ: [(0, 1), (0, 2), (0, 3), (2, 1), (0, 4), (2, 2), (2, 3), (1, 4)],
    MZ: [(0, -1), (0, -2), (0, -3), (2, -1), (2, -2), (2, -3), (2, 4)],
    PY: [(1, 0), (2, 0), (1, 1), (1, -1), (1, 2), (1, -2), (1, 3), (1, -3)],
    MY: [(-1, 0), (-1, 1), (-1, -1), (-1, 2), (-1, -2), (-1, 3), (-1, -3), (-1, 4)],
}
PARTS = (0, 1, 2, 3)
OVER_PARTS = (0, 1)
SPANS = ((0, 6), (6, 5), (OVER, 5), (OVER + 5, 5))
TREES = (((1, 1), False), ((1, -1), False), ((1, 1), True), ((-1, 1), True))


def wrap(o):
    return (o[0] % NY, o[1] % NZ)


def arrival_links():
    links = {}
    for p, ((sy, sz), moved) in enumerate(TREES):
        for d, order in CROSS.items():
            for turn, o in enumerate(order):
                d_here, turn_here = d, turn
                if moved and o == (-1, 4):
                    d_here, turn_here = MZ, len(order)
                links[wrap((sy * o[0], sz * o[1])), p] = (sy * d_here[0], sz * d_here[1]), turn_here
    return links


def plan(window, span, delay):
    links = arrival_links()
    todo = {d: sorted((k for k in links if links[k][0] == d), key=lambda k: (links[k][1], k[1])) for d in LINKS}
    here = {((0, 0), h) for h in PARTS}
    free = dict.fromkeys(LINKS, 0.0)
    flying = dict.fromkeys(LINKS, 0)
    arrivals = []

    def issue(now):
        sends = []
        for d in LINKS:
            for o, h in list(todo[d]):
                source = wrap((o[0] - d[0], o[1] - d[1]))
                if flying[d] < window and (source, h) in here:
                    todo[d].remove((o, h))
                    flying[d] += 1
                    free[d] = max(free[d], now) + span
                    arrivals.append((free[d] + delay, len(arrivals), d, o, h))
                    sends.append((source, h, d))
        return sends

    first = issue(0.0)
    turns = []
    while len(turns) < len(arrivals):
        now, _, d, o, h = sorted(arrivals)[len(turns)]
        here.add((o, h))
        flying[d] -= 1
        turns.append((o, h, issue(now)))
    return first, turns


FIRST, TURNS = plan(window=6, span=1.1, delay=2.0)
DONE = {o: i for i, (o, _, _) in enumerate(TURNS)}
ARRIVALS = [(0, 0)] + sorted(DONE, key=DONE.get)
PLACE = {o: i for i, o in enumerate(ARRIVALS)}
PIECES = 4
NEED = [1 + max(i for i, t in enumerate(TURNS) if PLACE[t[0]] < 8 * g + 8) for g in range(4)]
STEPS = 4 * PIECES


def handled(step):
    group, which = step // PIECES, step % PIECES
    if step < 0:
        return 0
    return NEED[group] + (NEED[min(group + 1, 3)] - NEED[group]) * which // PIECES


def kernel(
    trial_ref, slope_ref, offset_ref, trans_ref, out_ref,
    gath, slopes, offset, weights, sums, part, got, nodev, vals,
    local_sem, swap_send, swap_recv, yz_send, yz_recv, x_send, x_recv, a_send, a_recv, b_send, b_recv,
):
    node = lax.axis_index("node")
    cut = lax.axis_index("cut")
    x, core = node // 2, node % 2
    y, z = cut // NZ, cut % NZ
    odd = x % 2
    sibling = x * 2 + 1 - core
    share = 1 - core
    tiles = gath.shape[1]
    own_rows = slope_ref.shape[0]
    rows = gath.shape[2]
    fetch_at = odd * OVER
    mine_at = odd * FETCH
    other_at = (1 - odd) * FETCH
    beside = {d: ((y + d[0] + NY) % NY) * NZ + (z + d[1] + NZ) % NZ for d in LINKS}

    def part_of(o, h):
        at, count = SPANS[h]
        return gath.at[PLACE[o], pl.ds(at + mine_at if h in OVER_PARTS else at, count)]

    def yz_copy(o, h, d):
        oc = wrap((o[0] + d[0], o[1] + d[1]))
        return pltpu.make_async_remote_copy(
            src_ref=part_of(o, h), dst_ref=part_of(oc, h),
            send_sem=yz_send, recv_sem=yz_recv.at[PLACE[oc] - 1, h],
            device_id=(node, beside[d]), device_id_type=MESH,
        )

    def yz_arrived(o, h):
        ref = part_of(o, h)
        pltpu.make_async_copy(ref, ref, yz_recv.at[PLACE[o] - 1, h]).wait()

    def x_copy(o, h):
        ref = part_of(o, h)
        to = ((x + (1 if (PLACE[o] + h) % 2 else NX - 1)) % NX) * 2 + core
        return pltpu.make_async_remote_copy(
            src_ref=ref, dst_ref=ref, send_sem=x_send, recv_sem=x_recv.at[PLACE[o] // 8],
            device_id=(to, cut), device_id_type=MESH,
        )

    def x_arrived(group):
        low = max(8 * group, 1)
        ref = gath.at[pl.ds(low, 8 * group + 8 - low), pl.ds(other_at, OVER)]
        pltpu.make_async_copy(ref, ref, x_recv.at[group]).wait()

    def product(group, at, count, owner):
        low = owner * own_rows
        left = [gath[pl.ds(8 * group, 8), at + k].reshape(8 * rows, TILE) for k in range(count)]
        right = [slopes[at + k, pl.ds(low, own_rows), :] for k in range(count)]
        return lax.dot_general(
            jnp.concatenate(left, axis=1), jnp.concatenate(right, axis=1), (((1,), (1,)), ((), ())),
            preferred_element_type=jnp.float32,
        )

    def compute(piece):
        group = lax.div(piece, PIECES)
        which = lax.rem(piece, PIECES)
        owner = lax.rem(core + which, 2)

        @pl.when(which < 2)
        def _():
            sums[owner] = product(group, fetch_at, FETCH, owner)

        @pl.when(which >= 2)
        def _():
            rest = product(group, other_at, OVER, owner)
            lane = lax.broadcasted_iota(jnp.int32, (8 * rows, TILE), 1)
            best = jnp.zeros((8 * rows, TILE), jnp.float32)
            for n in range(4):
                at = slice(n * 128, n * 128 + 128)
                total = sums[owner, :, at] + rest[:, at] + offset[owner, n:n + 1, :]
                best = jnp.where(lane == n, jnp.max(total, axis=1, keepdims=True), best)
            turned = best.T
            part[2 * group, owner] = turned[0:4, 0:128]
            part[2 * group + 1, owner] = turned[0:4, 128:256]

    def tell(group):
        for i in range(max(8 * group, 1), 8 * group + 8):
            o = ARRIVALS[i]
            owner = ((y - o[0] + NY) % NY) * NZ + (z - o[1] + NZ) % NZ
            pltpu.make_async_remote_copy(
                src_ref=part.at[i // 4], dst_ref=got.at[i - 1], send_sem=a_send, recv_sem=a_recv,
                device_id=(node, owner), device_id_type=MESH,
            ).start()

    def column(k):
        return pl.ds(pl.multiple_of(k * TILE, TILE), TILE)

    def own(k, sem):
        return pltpu.make_async_copy(
            trial_ref.at[pl.ds(share * rows, rows), column(k)], gath.at[0, k], sem
        )

    own_parts = ((mine_at, OVER, local_sem.at[0]), (OVER, MIDDLE, local_sem.at[4]), (other_at, OVER, local_sem.at[5]))

    def own_arrived(i):
        at, count, sem = own_parts[i]
        ref = gath.at[0, pl.ds(at, count)]
        pltpu.make_async_copy(ref, ref, sem).wait()

    def load(k):
        return pltpu.make_async_copy(
            slope_ref.at[:, column(k)], slopes.at[k, pl.ds(core * own_rows, own_rows)], local_sem.at[1]
        )

    loaded = slopes.at[:, pl.ds(core * own_rows, own_rows)]
    load_offset = pltpu.make_async_copy(offset_ref, offset.at[core], local_sem.at[2])
    load_trans = pltpu.make_async_copy(trans_ref, weights, local_sem.at[3])
    swap = pltpu.make_async_remote_copy(
        src_ref=loaded, dst_ref=loaded, send_sem=swap_send.at[0], recv_sem=swap_recv.at[0],
        device_id=(sibling, cut), device_id_type=MESH,
    )
    swap_offset = pltpu.make_async_remote_copy(
        src_ref=offset_ref, dst_ref=offset.at[core],
        send_sem=swap_send.at[1], recv_sem=swap_recv.at[1],
        device_id=(sibling, cut), device_id_type=MESH,
    )
    barrier = pltpu.get_barrier_semaphore()
    for d in LINKS:
        pl.semaphore_signal(barrier, inc=1, device_id=(node, beside[d]), device_id_type=MESH)
    for j in range(1, 8):
        pl.semaphore_signal(barrier, inc=1, device_id=((node + j) % 8, cut), device_id_type=MESH)
    for at, count, sem in own_parts:
        for k in range(count):
            own(at + k, sem).start()
    load_offset.start()
    load_trans.start()
    pl.semaphore_wait(barrier, 11)
    own_arrived(0)
    for o, h, d in FIRST:
        if h in OVER_PARTS:
            yz_copy(o, h, d).start()
    own_arrived(1)
    for o, h, d in FIRST:
        if h not in OVER_PARTS:
            yz_copy(o, h, d).start()
    swap_offset.start()
    for k in range(tiles):
        load(k).start()
    pltpu.make_async_copy(loaded, loaded, local_sem.at[1]).wait()
    swap.start()

    def talk(k):
        for o, h, sends in TURNS[handled(k - 1):handled(k)]:
            yz_arrived(o, h)
            for send in sends:
                yz_copy(*send).start()
            if h in OVER_PARTS:
                x_copy(o, h).start()
        if k == 0:
            own_arrived(2)
            load_offset.wait()
        if k == 1:
            swap_offset.wait()
            swap.wait()
        if k % PIECES == 0 and k > 0:
            tell(k // PIECES - 1)
        if k % PIECES == PIECES // 2:
            x_arrived(k // PIECES)

    def choose(step, low, high):
        if high - low == 1:
            talk(low)
            return
        mid = (low + high) // 2

        @pl.when(step < mid)
        def _():
            choose(step, low, mid)

        @pl.when(step >= mid)
        def _():
            choose(step, mid, high)

    def turn(step, carry):
        choose(step, 0, STEPS)
        compute(step)
        return carry

    lax.fori_loop(0, STEPS, turn, 0)
    tell(3)

    for count, sem in ((FETCH, yz_send), (OVER, x_send)):
        ref = gath.at[pl.ds(0, len(ARRIVALS) - 1), pl.ds(0, count)]
        pltpu.make_async_copy(ref, ref, sem).wait()
    pltpu.make_async_copy(got, got, a_recv).wait()
    pltpu.make_async_copy(got, got, a_send).wait()
    best = None
    for q in range(4):
        tiles = [got[i - 1] for i in range(q, len(ARRIVALS), 4) if i > 0]
        if q == 0:
            tiles.append(part[0])
        top = functools.reduce(jnp.maximum, tiles)[:, :, q * rows:(q + 1) * rows]
        best = top if best is None else jnp.maximum(best, top)
    nodev[node, :, :, 0:rows] = best
    for j in range(4):
        to = 4 * share + j

        @pl.when(to != node)
        def _():
            pltpu.make_async_remote_copy(
                src_ref=nodev.at[node], dst_ref=nodev.at[node], send_sem=b_send, recv_sem=b_recv,
                device_id=(to, cut), device_id_type=MESH,
            ).start()

    load_trans.wait()
    trans = weights[...]
    mixing = trans / jnp.sum(trans, axis=1, keepdims=True)
    holder = 1 - node // 4
    keeps = holder == core

    @pl.when(keeps)
    def _():
        ref = nodev.at[pl.ds(0, 3)]
        pltpu.make_async_copy(ref, ref, b_recv).wait()
        pltpu.make_async_copy(ref, ref, b_send).wait()

    @pl.when(jnp.logical_not(keeps))
    def _():
        ref = nodev.at[pl.ds(0, 4)]
        pltpu.make_async_copy(ref, ref, b_recv).wait()
        pltpu.make_async_copy(ref, ref, b_send).wait()

    known = jnp.concatenate(
        [nodev[2 * i + holder, m, :, 0:rows] for i in range(NX) for m in range(2)], axis=0
    )
    vals[...] = lax.dot_general(
        known.T, mixing, (((1,), (1,)), ((), ())),
        precision=lax.Precision.HIGHEST, preferred_element_type=jnp.float32,
    )
    out_ref[0] = vals[pl.ds(pl.multiple_of((node % 4) * 8, 8), 8), :]


def per_device(trial_states, cut_slopes, cut_intercepts, transition):
    node_local, cut_local, width = cut_slopes.shape
    rows = trial_states.shape[0]
    nodes = transition.shape[0]
    slope_rows = cut_slopes.reshape(node_local * cut_local, width)
    count = len(ARRIVALS)
    sems = pltpu.SemaphoreType.DMA
    return pl.pallas_call(
        kernel,
        out_shape=jax.ShapeDtypeStruct((1, rows // 8, nodes), jnp.float32),
        in_specs=[pl.BlockSpec(memory_space=pltpu.HBM)] * 4,
        out_specs=pl.BlockSpec(memory_space=pltpu.VMEM),
        scratch_shapes=[
            pltpu.VMEM((count, width // TILE, rows // 2, TILE), jnp.bfloat16),
            pltpu.VMEM((width // TILE, 2 * node_local * cut_local, TILE), jnp.bfloat16),
            pltpu.VMEM((2, node_local, cut_local), jnp.float32),
            pltpu.VMEM(transition.shape, jnp.float32),
            pltpu.VMEM((2, 4 * rows, node_local * cut_local), jnp.float32),
            pltpu.VMEM((count // 4, 2, node_local, 128), jnp.float32),
            pltpu.VMEM((count - 1, 2, node_local, 128), jnp.float32),
            pltpu.VMEM((8, 2, node_local, 128), jnp.float32),
            pltpu.VMEM((rows // 2, nodes), jnp.float32),
            sems((6,)),
            sems((2,)),
            sems((2,)),
            sems(()),
            sems((count - 1, len(PARTS))),
            sems(()),
            sems((count // 8,)),
            sems(()),
            sems(()),
            sems(()),
            sems(()),
        ],
        compiler_params=pltpu.CompilerParams(
            collective_id=0, has_side_effects=True, vmem_limit_bytes=40 * 1024 * 1024
        ),
        cost_estimate=pl.CostEstimate(
            flops=2 * 512 * 2048 * 4096, bytes_accessed=5 * 1024 * 1024, transcendentals=0
        ),
    )(*[
        pltpu.with_memory_space_constraint(v, pltpu.HBM)
        for v in (trial_states, slope_rows, cut_intercepts, transition)
    ])


def solution(mesh):
    return jax.shard_map(
        per_device,
        mesh=mesh,
        in_specs=(P("cut", None), P("node", "cut", None), P("node", "cut"), P()),
        out_specs=P("cut", "node", None),
        check_vma=False,
    )
```

```python
import functools

import jax
import jax.numpy as jnp
from jax import lax
from jax.experimental import pallas as pl
from jax.experimental.pallas import tpu as pltpu
from jax.sharding import PartitionSpec as P

MESH = pl.DeviceIdType.MESH

NY, NZ, NX = 4, 8, 4

TILE, OVER, MIDDLE = 128, 11, 10
FETCH = OVER + MIDDLE

PZ, MZ, PY, MY = (0, 1), (0, -1), (1, 0), (-1, 0)
LINKS = (PZ, MZ, PY, MY)

CROSS = {
    PZ: [(0, 1), (0, 2), (0, 3), (2, 1), (0, 4), (2, 2), (2, 3), (1, 4)],
    MZ: [(0, -1), (0, -2), (0, -3), (2, -1), (2, -2), (2, -3), (2, 4)],
    PY: [(1, 0), (2, 0), (1, 1), (1, -1), (1, 2), (1, -2), (1, 3), (1, -3)],
    MY: [(-1, 0), (-1, 1), (-1, -1), (-1, 2), (-1, -2), (-1, 3), (-1, -3), (-1, 4)],
}
PARTS = (0, 1, 2, 3)
OVER_PARTS = (0, 1)
SPANS = ((0, 6), (6, 5), (OVER, 5), (OVER + 5, 5))
TREES = (((1, 1), False), ((1, -1), False), ((1, 1), True), ((-1, 1), True))


def wrap(o):
    return (o[0] % NY, o[1] % NZ)


def arrival_links():
    links = {}
    for p, ((sy, sz), moved) in enumerate(TREES):
        for d, order in CROSS.items():
            for turn, o in enumerate(order):
                d_here, turn_here = d, turn
                if moved and o == (-1, 4):
                    d_here, turn_here = MZ, len(order)
                links[wrap((sy * o[0], sz * o[1])), p] = (sy * d_here[0], sz * d_here[1]), turn_here
    return links


def plan(window, span, delay):
    links = arrival_links()
    todo = {d: sorted((k for k in links if links[k][0] == d), key=lambda k: (links[k][1], k[1])) for d in LINKS}
    here = {((0, 0), h) for h in PARTS}
    free = dict.fromkeys(LINKS, 0.0)
    flying = dict.fromkeys(LINKS, 0)
    arrivals = []

    def issue(now):
        sends = []
        for d in LINKS:
            for o, h in list(todo[d]):
                source = wrap((o[0] - d[0], o[1] - d[1]))
                if flying[d] < window and (source, h) in here:
                    todo[d].remove((o, h))
                    flying[d] += 1
                    free[d] = max(free[d], now) + span
                    arrivals.append((free[d] + delay, len(arrivals), d, o, h))
                    sends.append((source, h, d))
        return sends

    first = issue(0.0)
    turns = []
    while len(turns) < len(arrivals):
        now, _, d, o, h = sorted(arrivals)[len(turns)]
        here.add((o, h))
        flying[d] -= 1
        turns.append((o, h, issue(now)))
    return first, turns


FIRST, TURNS = plan(window=6, span=1.1, delay=2.0)
DONE = {o: i for i, (o, _, _) in enumerate(TURNS)}
ARRIVALS = [(0, 0)] + sorted(DONE, key=DONE.get)
PLACE = {o: i for i, o in enumerate(ARRIVALS)}
PIECES = 4
PACE = (0, 4, 12, 14)
NEED = [1 + max(i for i, t in enumerate(TURNS) if PLACE[t[0]] < 8 * g + 8) for g in range(4)]
STEPS = 4 * PIECES


def handled(step):
    group, which = step // PIECES, step % PIECES
    if step < 0:
        return 0
    return NEED[group] + (NEED[min(group + 1, 3)] - NEED[group]) * PACE[which] // 16


def kernel(
    trial_ref, slope_ref, offset_ref, trans_ref, out_ref,
    gath, slopes, offset, weights, sums, part, got, nodev, vals,
    local_sem, swap_send, swap_recv, yz_send, yz_recv, x_send, x_recv, a_send, a_recv, b_send, b_recv,
):
    node = lax.axis_index("node")
    cut = lax.axis_index("cut")
    x, core = node // 2, node % 2
    y, z = cut // NZ, cut % NZ
    odd = x % 2
    sibling = x * 2 + 1 - core
    share = 1 - core
    tiles = gath.shape[1]
    own_rows = slope_ref.shape[0]
    rows = gath.shape[2]
    fetch_at = odd * OVER
    mine_at = odd * FETCH
    other_at = (1 - odd) * FETCH
    beside = {d: ((y + d[0] + NY) % NY) * NZ + (z + d[1] + NZ) % NZ for d in LINKS}

    def part_of(o, h):
        at, count = SPANS[h]
        return gath.at[PLACE[o], pl.ds(at + mine_at if h in OVER_PARTS else at, count)]

    def yz_copy(o, h, d):
        oc = wrap((o[0] + d[0], o[1] + d[1]))
        return pltpu.make_async_remote_copy(
            src_ref=part_of(o, h), dst_ref=part_of(oc, h),
            send_sem=yz_send, recv_sem=yz_recv.at[PLACE[oc] - 1, h],
            device_id=(node, beside[d]), device_id_type=MESH,
        )

    def yz_arrived(o, h):
        ref = part_of(o, h)
        pltpu.make_async_copy(ref, ref, yz_recv.at[PLACE[o] - 1, h]).wait()

    def x_copy(o, h):
        ref = part_of(o, h)
        to = ((x + (1 if (PLACE[o] + h) % 2 else NX - 1)) % NX) * 2 + core
        return pltpu.make_async_remote_copy(
            src_ref=ref, dst_ref=ref, send_sem=x_send, recv_sem=x_recv.at[PLACE[o] // 8],
            device_id=(to, cut), device_id_type=MESH,
        )

    def x_arrived(group):
        low = max(8 * group, 1)
        ref = gath.at[pl.ds(low, 8 * group + 8 - low), pl.ds(other_at, OVER)]
        pltpu.make_async_copy(ref, ref, x_recv.at[group]).wait()

    def product(group, at, count, owner):
        low = owner * own_rows
        left = [gath[pl.ds(8 * group, 8), at + k].reshape(8 * rows, TILE) for k in range(count)]
        right = [slopes[at + k, pl.ds(low, own_rows), :] for k in range(count)]
        return lax.dot_general(
            jnp.concatenate(left, axis=1), jnp.concatenate(right, axis=1), (((1,), (1,)), ((), ())),
            preferred_element_type=jnp.float32,
        )

    def compute(piece):
        group = lax.div(piece, PIECES)
        which = lax.rem(piece, PIECES)
        owner = lax.rem(core + which, 2)

        @pl.when(which < 2)
        def _():
            sums[owner] = product(group, fetch_at, FETCH, owner)

        @pl.when(which >= 2)
        def _():
            rest = product(group, other_at, OVER, owner)
            lane = lax.broadcasted_iota(jnp.int32, (8 * rows, TILE), 1)
            best = jnp.zeros((8 * rows, TILE), jnp.float32)
            for n in range(4):
                at = slice(n * 128, n * 128 + 128)
                total = sums[owner, :, at] + rest[:, at] + offset[owner, n:n + 1, :]
                best = jnp.where(lane == n, jnp.max(total, axis=1, keepdims=True), best)
            turned = best.T
            part[2 * group, owner] = turned[0:4, 0:128]
            part[2 * group + 1, owner] = turned[0:4, 128:256]

    def tell(group):
        for i in range(max(8 * group, 1), 8 * group + 8):
            o = ARRIVALS[i]
            owner = ((y - o[0] + NY) % NY) * NZ + (z - o[1] + NZ) % NZ
            pltpu.make_async_remote_copy(
                src_ref=part.at[i // 4], dst_ref=got.at[i - 1], send_sem=a_send, recv_sem=a_recv,
                device_id=(node, owner), device_id_type=MESH,
            ).start()

    def column(k):
        return pl.ds(pl.multiple_of(k * TILE, TILE), TILE)

    def own(k, sem):
        return pltpu.make_async_copy(
            trial_ref.at[pl.ds(share * rows, rows), column(k)], gath.at[0, k], sem
        )

    own_parts = ((mine_at, OVER, local_sem.at[0]), (OVER, MIDDLE, local_sem.at[4]), (other_at, OVER, local_sem.at[5]))

    def own_arrived(i):
        at, count, sem = own_parts[i]
        ref = gath.at[0, pl.ds(at, count)]
        pltpu.make_async_copy(ref, ref, sem).wait()

    def load(k):
        return pltpu.make_async_copy(
            slope_ref.at[:, column(k)], slopes.at[k, pl.ds(core * own_rows, own_rows)], local_sem.at[1]
        )

    loaded = slopes.at[:, pl.ds(core * own_rows, own_rows)]
    load_offset = pltpu.make_async_copy(offset_ref, offset.at[core], local_sem.at[2])
    load_trans = pltpu.make_async_copy(trans_ref, weights, local_sem.at[3])
    swap = pltpu.make_async_remote_copy(
        src_ref=loaded, dst_ref=loaded, send_sem=swap_send.at[0], recv_sem=swap_recv.at[0],
        device_id=(sibling, cut), device_id_type=MESH,
    )
    swap_offset = pltpu.make_async_remote_copy(
        src_ref=offset_ref, dst_ref=offset.at[core],
        send_sem=swap_send.at[1], recv_sem=swap_recv.at[1],
        device_id=(sibling, cut), device_id_type=MESH,
    )
    barrier = pltpu.get_barrier_semaphore()
    for d in LINKS:
        pl.semaphore_signal(barrier, inc=1, device_id=(node, beside[d]), device_id_type=MESH)
    for j in range(1, 8):
        pl.semaphore_signal(barrier, inc=1, device_id=((node + j) % 8, cut), device_id_type=MESH)
    for at, count, sem in own_parts:
        for k in range(count):
            own(at + k, sem).start()
    load_offset.start()
    load_trans.start()
    pl.semaphore_wait(barrier, 11)
    own_arrived(0)
    for o, h, d in FIRST:
        if h in OVER_PARTS:
            yz_copy(o, h, d).start()
    own_arrived(1)
    for o, h, d in FIRST:
        if h not in OVER_PARTS:
            yz_copy(o, h, d).start()
    swap_offset.start()
    for k in range(tiles):
        load(k).start()
    pltpu.make_async_copy(loaded, loaded, local_sem.at[1]).wait()
    swap.start()

    def talk(k):
        for o, h, sends in TURNS[handled(k - 1):handled(k)]:
            yz_arrived(o, h)
            for send in sends:
                yz_copy(*send).start()
            if h in OVER_PARTS:
                x_copy(o, h).start()
        if k == 0:
            own_arrived(2)
            load_offset.wait()
        if k == 1:
            swap_offset.wait()
            swap.wait()
        if k % PIECES == 0 and k > 0:
            tell(k // PIECES - 1)
        if k % PIECES == PIECES // 2:
            x_arrived(k // PIECES)

    def choose(step, low, high):
        if high - low == 1:
            talk(low)
            return
        mid = (low + high) // 2

        @pl.when(step < mid)
        def _():
            choose(step, low, mid)

        @pl.when(step >= mid)
        def _():
            choose(step, mid, high)

    def turn(step, carry):
        choose(step, 0, STEPS)
        compute(step)
        return carry

    lax.fori_loop(0, STEPS, turn, 0)
    tell(3)

    for count, sem in ((FETCH, yz_send), (OVER, x_send)):
        ref = gath.at[pl.ds(0, len(ARRIVALS) - 1), pl.ds(0, count)]
        pltpu.make_async_copy(ref, ref, sem).wait()
    pltpu.make_async_copy(got, got, a_recv).wait()
    pltpu.make_async_copy(got, got, a_send).wait()
    best = None
    for q in range(4):
        tiles = [got[i - 1] for i in range(q, len(ARRIVALS), 4) if i > 0]
        if q == 0:
            tiles.append(part[0])
        top = functools.reduce(jnp.maximum, tiles)[:, :, q * rows:(q + 1) * rows]
        best = top if best is None else jnp.maximum(best, top)
    nodev[node, :, :, 0:rows] = best
    for j in range(4):
        to = 4 * share + j

        @pl.when(to != node)
        def _():
            pltpu.make_async_remote_copy(
                src_ref=nodev.at[node], dst_ref=nodev.at[node], send_sem=b_send, recv_sem=b_recv,
                device_id=(to, cut), device_id_type=MESH,
            ).start()

    load_trans.wait()
    trans = weights[...]
    mixing = trans / jnp.sum(trans, axis=1, keepdims=True)
    holder = 1 - node // 4
    keeps = holder == core

    @pl.when(keeps)
    def _():
        ref = nodev.at[pl.ds(0, 3)]
        pltpu.make_async_copy(ref, ref, b_recv).wait()
        pltpu.make_async_copy(ref, ref, b_send).wait()

    @pl.when(jnp.logical_not(keeps))
    def _():
        ref = nodev.at[pl.ds(0, 4)]
        pltpu.make_async_copy(ref, ref, b_recv).wait()
        pltpu.make_async_copy(ref, ref, b_send).wait()

    known = jnp.concatenate(
        [nodev[2 * i + holder, m, :, 0:rows] for i in range(NX) for m in range(2)], axis=0
    )
    vals[...] = lax.dot_general(
        known.T, mixing, (((1,), (1,)), ((), ())),
        precision=lax.Precision.HIGHEST, preferred_element_type=jnp.float32,
    )
    out_ref[0] = vals[pl.ds(pl.multiple_of((node % 4) * 8, 8), 8), :]


def per_device(trial_states, cut_slopes, cut_intercepts, transition):
    node_local, cut_local, width = cut_slopes.shape
    rows = trial_states.shape[0]
    nodes = transition.shape[0]
    slope_rows = cut_slopes.reshape(node_local * cut_local, width)
    count = len(ARRIVALS)
    sems = pltpu.SemaphoreType.DMA
    return pl.pallas_call(
        kernel,
        out_shape=jax.ShapeDtypeStruct((1, rows // 8, nodes), jnp.float32),
        in_specs=[pl.BlockSpec(memory_space=pltpu.HBM)] * 4,
        out_specs=pl.BlockSpec(memory_space=pltpu.VMEM),
        scratch_shapes=[
            pltpu.VMEM((count, width // TILE, rows // 2, TILE), jnp.bfloat16),
            pltpu.VMEM((width // TILE, 2 * node_local * cut_local, TILE), jnp.bfloat16),
            pltpu.VMEM((2, node_local, cut_local), jnp.float32),
            pltpu.VMEM(transition.shape, jnp.float32),
            pltpu.VMEM((2, 4 * rows, node_local * cut_local), jnp.float32),
            pltpu.VMEM((count // 4, 2, node_local, 128), jnp.float32),
            pltpu.VMEM((count - 1, 2, node_local, 128), jnp.float32),
            pltpu.VMEM((8, 2, node_local, 128), jnp.float32),
            pltpu.VMEM((rows // 2, nodes), jnp.float32),
            sems((6,)),
            sems((2,)),
            sems((2,)),
            sems(()),
            sems((count - 1, len(PARTS))),
            sems(()),
            sems((count // 8,)),
            sems(()),
            sems(()),
            sems(()),
            sems(()),
        ],
        compiler_params=pltpu.CompilerParams(
            collective_id=0, has_side_effects=True, vmem_limit_bytes=40 * 1024 * 1024
        ),
        cost_estimate=pl.CostEstimate(
            flops=2 * 512 * 2048 * 4096, bytes_accessed=5 * 1024 * 1024, transcendentals=0
        ),
    )(*[
        pltpu.with_memory_space_constraint(v, pltpu.HBM)
        for v in (trial_states, slope_rows, cut_intercepts, transition)
    ])


def solution(mesh):
    return jax.shard_map(
        per_device,
        mesh=mesh,
        in_specs=(P("cut", None), P("node", "cut", None), P("node", "cut"), P()),
        out_specs=P("cut", "node", None),
        check_vma=False,
    )
```

```python
import functools

import jax
import jax.numpy as jnp
from jax import lax
from jax.experimental import pallas as pl
from jax.experimental.pallas import tpu as pltpu
from jax.sharding import PartitionSpec as P

MESH = pl.DeviceIdType.MESH

NY, NZ, NX = 4, 8, 4

TILE, OVER, MIDDLE = 128, 11, 10
FETCH = OVER + MIDDLE

PZ, MZ, PY, MY = (0, 1), (0, -1), (1, 0), (-1, 0)
LINKS = (PZ, MZ, PY, MY)

CROSS = {
    PZ: [(0, 1), (0, 2), (0, 3), (2, 1), (0, 4), (2, 2), (2, 3), (1, 4)],
    MZ: [(0, -1), (0, -2), (0, -3), (2, -1), (2, -2), (2, -3), (2, 4)],
    PY: [(1, 0), (2, 0), (1, 1), (1, -1), (1, 2), (1, -2), (1, 3), (1, -3)],
    MY: [(-1, 0), (-1, 1), (-1, -1), (-1, 2), (-1, -2), (-1, 3), (-1, -3), (-1, 4)],
}
PARTS = (0, 1, 2, 3)
OVER_PARTS = (0, 1)
SPANS = ((0, 6), (6, 5), (OVER, 5), (OVER + 5, 5))
TREES = (((1, 1), False), ((1, -1), False), ((1, 1), True), ((-1, 1), True))


def wrap(o):
    return (o[0] % NY, o[1] % NZ)


def arrival_links():
    links = {}
    for p, ((sy, sz), moved) in enumerate(TREES):
        for d, order in CROSS.items():
            for turn, o in enumerate(order):
                d_here, turn_here = d, turn
                if moved and o == (-1, 4):
                    d_here, turn_here = MZ, len(order)
                links[wrap((sy * o[0], sz * o[1])), p] = (sy * d_here[0], sz * d_here[1]), turn_here
    return links


def plan(window, span, delay):
    links = arrival_links()
    todo = {
        d: sorted(
            (k for k in links if links[k][0] == d), key=lambda k: (links[k][1] + (k[1] not in OVER_PARTS), k[1])
        )
        for d in LINKS
    }
    here = {((0, 0), h) for h in PARTS}
    free = dict.fromkeys(LINKS, 0.0)
    flying = dict.fromkeys(LINKS, 0)
    arrivals = []

    def issue(now):
        sends = []
        for d in LINKS:
            for o, h in list(todo[d]):
                source = wrap((o[0] - d[0], o[1] - d[1]))
                if flying[d] < window and (source, h) in here:
                    todo[d].remove((o, h))
                    flying[d] += 1
                    free[d] = max(free[d], now) + span
                    arrivals.append((free[d] + delay, len(arrivals), d, o, h))
                    sends.append((source, h, d))
        return sends

    first = issue(0.0)
    turns = []
    while len(turns) < len(arrivals):
        now, _, d, o, h = sorted(arrivals)[len(turns)]
        here.add((o, h))
        flying[d] -= 1
        turns.append((o, h, issue(now)))
    return first, turns


FIRST, TURNS = plan(window=6, span=1.1, delay=2.0)
DONE = {o: i for i, (o, _, _) in enumerate(TURNS)}
ARRIVALS = [(0, 0)] + sorted(DONE, key=DONE.get)
PLACE = {o: i for i, o in enumerate(ARRIVALS)}
PIECES = 4
PACE = (0, 4, 12, 14)
NEED = [1 + max(i for i, t in enumerate(TURNS) if PLACE[t[0]] < 8 * g + 8) for g in range(4)]
STEPS = 4 * PIECES


def handled(step):
    group, which = step // PIECES, step % PIECES
    if step < 0:
        return 0
    return NEED[group] + (NEED[min(group + 1, 3)] - NEED[group]) * PACE[which] // 16


def kernel(
    trial_ref, slope_ref, offset_ref, trans_ref, out_ref,
    gath, slopes, offset, weights, sums, part, got, nodev, vals,
    local_sem, swap_send, swap_recv, yz_send, yz_recv, x_send, x_recv, a_send, a_recv, b_send, b_recv,
):
    node = lax.axis_index("node")
    cut = lax.axis_index("cut")
    x, core = node // 2, node % 2
    y, z = cut // NZ, cut % NZ
    odd = x % 2
    sibling = x * 2 + 1 - core
    share = 1 - core
    tiles = gath.shape[1]
    own_rows = slope_ref.shape[0]
    rows = gath.shape[2]
    fetch_at = odd * OVER
    mine_at = odd * FETCH
    other_at = (1 - odd) * FETCH
    beside = {d: ((y + d[0] + NY) % NY) * NZ + (z + d[1] + NZ) % NZ for d in LINKS}

    def part_of(o, h):
        at, count = SPANS[h]
        return gath.at[PLACE[o], pl.ds(at + mine_at if h in OVER_PARTS else at, count)]

    def yz_copy(o, h, d):
        oc = wrap((o[0] + d[0], o[1] + d[1]))
        return pltpu.make_async_remote_copy(
            src_ref=part_of(o, h), dst_ref=part_of(oc, h),
            send_sem=yz_send, recv_sem=yz_recv.at[PLACE[oc] - 1, h],
            device_id=(node, beside[d]), device_id_type=MESH,
        )

    def yz_arrived(o, h):
        ref = part_of(o, h)
        pltpu.make_async_copy(ref, ref, yz_recv.at[PLACE[o] - 1, h]).wait()

    def x_copy(o, h):
        ref = part_of(o, h)
        to = ((x + (1 if (PLACE[o] + h) % 2 else NX - 1)) % NX) * 2 + core
        return pltpu.make_async_remote_copy(
            src_ref=ref, dst_ref=ref, send_sem=x_send, recv_sem=x_recv.at[PLACE[o] // 8],
            device_id=(to, cut), device_id_type=MESH,
        )

    def x_arrived(group):
        low = max(8 * group, 1)
        ref = gath.at[pl.ds(low, 8 * group + 8 - low), pl.ds(other_at, OVER)]
        pltpu.make_async_copy(ref, ref, x_recv.at[group]).wait()

    def product(group, at, count, owner):
        low = owner * own_rows
        left = [gath[pl.ds(8 * group, 8), at + k].reshape(8 * rows, TILE) for k in range(count)]
        right = [slopes[at + k, pl.ds(low, own_rows), :] for k in range(count)]
        return lax.dot_general(
            jnp.concatenate(left, axis=1), jnp.concatenate(right, axis=1), (((1,), (1,)), ((), ())),
            preferred_element_type=jnp.float32,
        )

    def compute(piece):
        group = lax.div(piece, PIECES)
        which = lax.rem(piece, PIECES)
        owner = lax.rem(core + which, 2)

        @pl.when(which < 2)
        def _():
            sums[owner] = product(group, fetch_at, FETCH, owner)

        @pl.when(which >= 2)
        def _():
            rest = product(group, other_at, OVER, owner)
            lane = lax.broadcasted_iota(jnp.int32, (8 * rows, TILE), 1)
            best = jnp.zeros((8 * rows, TILE), jnp.float32)
            for n in range(4):
                at = slice(n * 128, n * 128 + 128)
                total = sums[owner, :, at] + rest[:, at] + offset[owner, n:n + 1, :]
                best = jnp.where(lane == n, jnp.max(total, axis=1, keepdims=True), best)
            turned = best.T
            part[2 * group, owner] = turned[0:4, 0:128]
            part[2 * group + 1, owner] = turned[0:4, 128:256]

    def tell(group):
        for i in range(max(8 * group, 1), 8 * group + 8):
            o = ARRIVALS[i]
            owner = ((y - o[0] + NY) % NY) * NZ + (z - o[1] + NZ) % NZ
            pltpu.make_async_remote_copy(
                src_ref=part.at[i // 4], dst_ref=got.at[i - 1], send_sem=a_send, recv_sem=a_recv,
                device_id=(node, owner), device_id_type=MESH,
            ).start()

    def column(k):
        return pl.ds(pl.multiple_of(k * TILE, TILE), TILE)

    def own(k, sem):
        return pltpu.make_async_copy(
            trial_ref.at[pl.ds(share * rows, rows), column(k)], gath.at[0, k], sem
        )

    own_parts = ((mine_at, OVER, local_sem.at[0]), (OVER, MIDDLE, local_sem.at[4]), (other_at, OVER, local_sem.at[5]))

    def own_arrived(i):
        at, count, sem = own_parts[i]
        ref = gath.at[0, pl.ds(at, count)]
        pltpu.make_async_copy(ref, ref, sem).wait()

    def load(k):
        return pltpu.make_async_copy(
            slope_ref.at[:, column(k)], slopes.at[k, pl.ds(core * own_rows, own_rows)], local_sem.at[1]
        )

    loaded = slopes.at[:, pl.ds(core * own_rows, own_rows)]
    load_offset = pltpu.make_async_copy(offset_ref, offset.at[core], local_sem.at[2])
    load_trans = pltpu.make_async_copy(trans_ref, weights, local_sem.at[3])
    swap = pltpu.make_async_remote_copy(
        src_ref=loaded, dst_ref=loaded, send_sem=swap_send.at[0], recv_sem=swap_recv.at[0],
        device_id=(sibling, cut), device_id_type=MESH,
    )
    swap_offset = pltpu.make_async_remote_copy(
        src_ref=offset_ref, dst_ref=offset.at[core],
        send_sem=swap_send.at[1], recv_sem=swap_recv.at[1],
        device_id=(sibling, cut), device_id_type=MESH,
    )
    barrier = pltpu.get_barrier_semaphore()
    for d in LINKS:
        pl.semaphore_signal(barrier, inc=1, device_id=(node, beside[d]), device_id_type=MESH)
    for j in range(1, 8):
        pl.semaphore_signal(barrier, inc=1, device_id=((node + j) % 8, cut), device_id_type=MESH)
    for at, count, sem in own_parts:
        for k in range(count):
            own(at + k, sem).start()
    load_offset.start()
    load_trans.start()
    pl.semaphore_wait(barrier, 11)
    own_arrived(0)
    for o, h, d in FIRST:
        if h in OVER_PARTS:
            yz_copy(o, h, d).start()
    own_arrived(1)
    for o, h, d in FIRST:
        if h not in OVER_PARTS:
            yz_copy(o, h, d).start()
    swap_offset.start()
    for k in range(tiles):
        load(k).start()
    pltpu.make_async_copy(loaded, loaded, local_sem.at[1]).wait()
    swap.start()

    def talk(k):
        for o, h, sends in TURNS[handled(k - 1):handled(k)]:
            yz_arrived(o, h)
            for send in sends:
                yz_copy(*send).start()
            if h in OVER_PARTS:
                x_copy(o, h).start()
        if k == 0:
            own_arrived(2)
            load_offset.wait()
        if k == 1:
            swap_offset.wait()
            swap.wait()
        if k % PIECES == 0 and k > 0:
            tell(k // PIECES - 1)
        if k % PIECES == PIECES // 2:
            x_arrived(k // PIECES)

    def choose(step, low, high):
        if high - low == 1:
            talk(low)
            return
        mid = (low + high) // 2

        @pl.when(step < mid)
        def _():
            choose(step, low, mid)

        @pl.when(step >= mid)
        def _():
            choose(step, mid, high)

    def turn(step, carry):
        choose(step, 0, STEPS)
        compute(step)
        return carry

    lax.fori_loop(0, STEPS, turn, 0)
    tell(3)

    for count, sem in ((FETCH, yz_send), (OVER, x_send)):
        ref = gath.at[pl.ds(0, len(ARRIVALS) - 1), pl.ds(0, count)]
        pltpu.make_async_copy(ref, ref, sem).wait()
    pltpu.make_async_copy(got, got, a_recv).wait()
    pltpu.make_async_copy(got, got, a_send).wait()
    best = None
    for q in range(4):
        tiles = [got[i - 1] for i in range(q, len(ARRIVALS), 4) if i > 0]
        if q == 0:
            tiles.append(part[0])
        top = functools.reduce(jnp.maximum, tiles)[:, :, q * rows:(q + 1) * rows]
        best = top if best is None else jnp.maximum(best, top)
    nodev[node, :, :, 0:rows] = best
    for j in range(4):
        to = 4 * share + j

        @pl.when(to != node)
        def _():
            pltpu.make_async_remote_copy(
                src_ref=nodev.at[node], dst_ref=nodev.at[node], send_sem=b_send, recv_sem=b_recv,
                device_id=(to, cut), device_id_type=MESH,
            ).start()

    load_trans.wait()
    trans = weights[...]
    mixing = trans / jnp.sum(trans, axis=1, keepdims=True)
    holder = 1 - node // 4
    keeps = holder == core

    @pl.when(keeps)
    def _():
        ref = nodev.at[pl.ds(0, 3)]
        pltpu.make_async_copy(ref, ref, b_recv).wait()
        pltpu.make_async_copy(ref, ref, b_send).wait()

    @pl.when(jnp.logical_not(keeps))
    def _():
        ref = nodev.at[pl.ds(0, 4)]
        pltpu.make_async_copy(ref, ref, b_recv).wait()
        pltpu.make_async_copy(ref, ref, b_send).wait()

    known = jnp.concatenate(
        [nodev[2 * i + holder, m, :, 0:rows] for i in range(NX) for m in range(2)], axis=0
    )
    vals[...] = lax.dot_general(
        known.T, mixing, (((1,), (1,)), ((), ())),
        precision=lax.Precision.HIGHEST, preferred_element_type=jnp.float32,
    )
    out_ref[0] = vals[pl.ds(pl.multiple_of((node % 4) * 8, 8), 8), :]


def per_device(trial_states, cut_slopes, cut_intercepts, transition):
    node_local, cut_local, width = cut_slopes.shape
    rows = trial_states.shape[0]
    nodes = transition.shape[0]
    slope_rows = cut_slopes.reshape(node_local * cut_local, width)
    count = len(ARRIVALS)
    sems = pltpu.SemaphoreType.DMA
    return pl.pallas_call(
        kernel,
        out_shape=jax.ShapeDtypeStruct((1, rows // 8, nodes), jnp.float32),
        in_specs=[pl.BlockSpec(memory_space=pltpu.HBM)] * 4,
        out_specs=pl.BlockSpec(memory_space=pltpu.VMEM),
        scratch_shapes=[
            pltpu.VMEM((count, width // TILE, rows // 2, TILE), jnp.bfloat16),
            pltpu.VMEM((width // TILE, 2 * node_local * cut_local, TILE), jnp.bfloat16),
            pltpu.VMEM((2, node_local, cut_local), jnp.float32),
            pltpu.VMEM(transition.shape, jnp.float32),
            pltpu.VMEM((2, 4 * rows, node_local * cut_local), jnp.float32),
            pltpu.VMEM((count // 4, 2, node_local, 128), jnp.float32),
            pltpu.VMEM((count - 1, 2, node_local, 128), jnp.float32),
            pltpu.VMEM((8, 2, node_local, 128), jnp.float32),
            pltpu.VMEM((rows // 2, nodes), jnp.float32),
            sems((6,)),
            sems((2,)),
            sems((2,)),
            sems(()),
            sems((count - 1, len(PARTS))),
            sems(()),
            sems((count // 8,)),
            sems(()),
            sems(()),
            sems(()),
            sems(()),
        ],
        compiler_params=pltpu.CompilerParams(
            collective_id=0, has_side_effects=True, vmem_limit_bytes=40 * 1024 * 1024
        ),
        cost_estimate=pl.CostEstimate(
            flops=2 * 512 * 2048 * 4096, bytes_accessed=5 * 1024 * 1024, transcendentals=0
        ),
    )(*[
        pltpu.with_memory_space_constraint(v, pltpu.HBM)
        for v in (trial_states, slope_rows, cut_intercepts, transition)
    ])


def solution(mesh):
    return jax.shard_map(
        per_device,
        mesh=mesh,
        in_specs=(P("cut", None), P("node", "cut", None), P("node", "cut"), P()),
        out_specs=P("cut", "node", None),
        check_vma=False,
    )
```

```python
import functools

import jax
import jax.numpy as jnp
from jax import lax
from jax.experimental import pallas as pl
from jax.experimental.pallas import tpu as pltpu
from jax.sharding import PartitionSpec as P

MESH = pl.DeviceIdType.MESH

NY, NZ, NX = 4, 8, 4

TILE, OVER, MIDDLE = 128, 11, 10
FETCH = OVER + MIDDLE

PZ, MZ, PY, MY = (0, 1), (0, -1), (1, 0), (-1, 0)
LINKS = (PZ, MZ, PY, MY)

CROSS = {
    PZ: [(0, 1), (0, 2), (0, 3), (2, 1), (0, 4), (2, 2), (2, 3), (1, 4)],
    MZ: [(0, -1), (0, -2), (0, -3), (2, -1), (2, -2), (2, -3), (2, 4)],
    PY: [(1, 0), (2, 0), (1, 1), (1, -1), (1, 2), (1, -2), (1, 3), (1, -3)],
    MY: [(-1, 0), (-1, 1), (-1, -1), (-1, 2), (-1, -2), (-1, 3), (-1, -3), (-1, 4)],
}
PARTS = (0, 1, 2, 3)
OVER_PARTS = (0, 1)
SPANS = ((0, 6), (6, 5), (OVER, 5), (OVER + 5, 5))
MOVED = ({}, {(0, 4): (MZ, 3.5)}, {(-1, 4): (MZ, 7)}, {(1, -3): (MZ, 7)})


def wrap(o):
    return (o[0] % NY, o[1] % NZ)


def arrival_links():
    links = {}
    for p, moved in enumerate(MOVED):
        for d, order in CROSS.items():
            for turn, o in enumerate(order):
                links[wrap(o), p] = moved.get(o, (d, turn))
    return links


def plan(window, span, delay):
    links = arrival_links()
    todo = {d: sorted((k for k in links if links[k][0] == d), key=lambda k: (links[k][1], k[1])) for d in LINKS}
    here = {((0, 0), h) for h in PARTS}
    free = dict.fromkeys(LINKS, 0.0)
    flying = dict.fromkeys(LINKS, 0)
    arrivals = []

    def issue(now):
        sends = []
        for d in LINKS:
            for o, h in list(todo[d]):
                source = wrap((o[0] - d[0], o[1] - d[1]))
                if flying[d] < window and (source, h) in here:
                    todo[d].remove((o, h))
                    flying[d] += 1
                    free[d] = max(free[d], now) + span
                    arrivals.append((free[d] + delay, len(arrivals), d, o, h))
                    sends.append((source, h, d))
        return sends

    first = issue(0.0)
    turns = []
    while len(turns) < len(arrivals):
        now, _, d, o, h = sorted(arrivals)[len(turns)]
        here.add((o, h))
        flying[d] -= 1
        turns.append((o, h, issue(now)))
    return first, turns


FIRST, TURNS = plan(window=6, span=1.1, delay=2.0)
DONE = {o: i for i, (o, _, _) in enumerate(TURNS)}
ARRIVALS = [(0, 0)] + sorted(DONE, key=DONE.get)
PLACE = {o: i for i, o in enumerate(ARRIVALS)}
PIECES = 4
PACE = (0, 4, 12, 14)
NEED = [1 + max(i for i, t in enumerate(TURNS) if PLACE[t[0]] < 8 * g + 8) for g in range(4)]
STEPS = 4 * PIECES


def handled(step):
    group, which = step // PIECES, step % PIECES
    if step < 0:
        return 0
    return NEED[group] + (NEED[min(group + 1, 3)] - NEED[group]) * PACE[which] // 16


def kernel(
    trial_ref, slope_ref, offset_ref, trans_ref, out_ref,
    gath, slopes, offset, weights, sums, part, got, nodev, vals,
    local_sem, swap_send, swap_recv, yz_send, yz_recv, x_send, x_recv, a_send, a_recv, b_send, b_recv,
):
    node = lax.axis_index("node")
    cut = lax.axis_index("cut")
    x, core = node // 2, node % 2
    y, z = cut // NZ, cut % NZ
    odd = x % 2
    sibling = x * 2 + 1 - core
    share = 1 - core
    tiles = gath.shape[1]
    own_rows = slope_ref.shape[0]
    rows = gath.shape[2]
    fetch_at = odd * OVER
    mine_at = odd * FETCH
    other_at = (1 - odd) * FETCH
    beside = {d: ((y + d[0] + NY) % NY) * NZ + (z + d[1] + NZ) % NZ for d in LINKS}

    def part_of(o, h):
        at, count = SPANS[h]
        return gath.at[PLACE[o], pl.ds(at + mine_at if h in OVER_PARTS else at, count)]

    def yz_copy(o, h, d):
        oc = wrap((o[0] + d[0], o[1] + d[1]))
        return pltpu.make_async_remote_copy(
            src_ref=part_of(o, h), dst_ref=part_of(oc, h),
            send_sem=yz_send, recv_sem=yz_recv.at[PLACE[oc] - 1, h],
            device_id=(node, beside[d]), device_id_type=MESH,
        )

    def yz_arrived(o, h):
        ref = part_of(o, h)
        pltpu.make_async_copy(ref, ref, yz_recv.at[PLACE[o] - 1, h]).wait()

    def x_copy(o, h):
        ref = part_of(o, h)
        to = ((x + (1 if (PLACE[o] + h) % 2 else NX - 1)) % NX) * 2 + core
        return pltpu.make_async_remote_copy(
            src_ref=ref, dst_ref=ref, send_sem=x_send, recv_sem=x_recv.at[PLACE[o] // 8],
            device_id=(to, cut), device_id_type=MESH,
        )

    def x_arrived(group):
        low = max(8 * group, 1)
        ref = gath.at[pl.ds(low, 8 * group + 8 - low), pl.ds(other_at, OVER)]
        pltpu.make_async_copy(ref, ref, x_recv.at[group]).wait()

    def product(group, at, count, owner):
        low = owner * own_rows
        left = [gath[pl.ds(8 * group, 8), at + k].reshape(8 * rows, TILE) for k in range(count)]
        right = [slopes[at + k, pl.ds(low, own_rows), :] for k in range(count)]
        return lax.dot_general(
            jnp.concatenate(left, axis=1), jnp.concatenate(right, axis=1), (((1,), (1,)), ((), ())),
            preferred_element_type=jnp.float32,
        )

    def compute(piece):
        group = lax.div(piece, PIECES)
        which = lax.rem(piece, PIECES)
        owner = lax.rem(core + which, 2)

        @pl.when(which < 2)
        def _():
            sums[owner] = product(group, fetch_at, FETCH, owner)

        @pl.when(which >= 2)
        def _():
            rest = product(group, other_at, OVER, owner)
            lane = lax.broadcasted_iota(jnp.int32, (8 * rows, TILE), 1)
            best = jnp.zeros((8 * rows, TILE), jnp.float32)
            for n in range(4):
                at = slice(n * 128, n * 128 + 128)
                total = sums[owner, :, at] + rest[:, at] + offset[owner, n:n + 1, :]
                best = jnp.where(lane == n, jnp.max(total, axis=1, keepdims=True), best)
            turned = best.T
            part[2 * group, owner] = turned[0:4, 0:128]
            part[2 * group + 1, owner] = turned[0:4, 128:256]

    def tell(group):
        for i in range(max(8 * group, 1), 8 * group + 8):
            o = ARRIVALS[i]
            owner = ((y - o[0] + NY) % NY) * NZ + (z - o[1] + NZ) % NZ
            pltpu.make_async_remote_copy(
                src_ref=part.at[i // 4], dst_ref=got.at[i - 1], send_sem=a_send, recv_sem=a_recv,
                device_id=(node, owner), device_id_type=MESH,
            ).start()

    def column(k):
        return pl.ds(pl.multiple_of(k * TILE, TILE), TILE)

    def own(k, sem):
        return pltpu.make_async_copy(
            trial_ref.at[pl.ds(share * rows, rows), column(k)], gath.at[0, k], sem
        )

    own_parts = ((mine_at, OVER, local_sem.at[0]), (OVER, MIDDLE, local_sem.at[4]), (other_at, OVER, local_sem.at[5]))

    def own_arrived(i):
        at, count, sem = own_parts[i]
        ref = gath.at[0, pl.ds(at, count)]
        pltpu.make_async_copy(ref, ref, sem).wait()

    def load(k):
        return pltpu.make_async_copy(
            slope_ref.at[:, column(k)], slopes.at[k, pl.ds(core * own_rows, own_rows)], local_sem.at[1]
        )

    loaded = slopes.at[:, pl.ds(core * own_rows, own_rows)]
    load_offset = pltpu.make_async_copy(offset_ref, offset.at[core], local_sem.at[2])
    load_trans = pltpu.make_async_copy(trans_ref, weights, local_sem.at[3])
    swap = pltpu.make_async_remote_copy(
        src_ref=loaded, dst_ref=loaded, send_sem=swap_send.at[0], recv_sem=swap_recv.at[0],
        device_id=(sibling, cut), device_id_type=MESH,
    )
    swap_offset = pltpu.make_async_remote_copy(
        src_ref=offset_ref, dst_ref=offset.at[core],
        send_sem=swap_send.at[1], recv_sem=swap_recv.at[1],
        device_id=(sibling, cut), device_id_type=MESH,
    )
    barrier = pltpu.get_barrier_semaphore()
    for d in LINKS:
        pl.semaphore_signal(barrier, inc=1, device_id=(node, beside[d]), device_id_type=MESH)
    for j in range(1, 8):
        pl.semaphore_signal(barrier, inc=1, device_id=((node + j) % 8, cut), device_id_type=MESH)
    for at, count, sem in own_parts:
        for k in range(count):
            own(at + k, sem).start()
    load_offset.start()
    load_trans.start()
    pl.semaphore_wait(barrier, 11)
    own_arrived(0)
    for o, h, d in FIRST:
        if h in OVER_PARTS:
            yz_copy(o, h, d).start()
    own_arrived(1)
    for o, h, d in FIRST:
        if h not in OVER_PARTS:
            yz_copy(o, h, d).start()
    swap_offset.start()
    for k in range(tiles):
        load(k).start()
    pltpu.make_async_copy(loaded, loaded, local_sem.at[1]).wait()
    swap.start()

    def talk(k):
        for o, h, sends in TURNS[handled(k - 1):handled(k)]:
            yz_arrived(o, h)
            for send in sends:
                yz_copy(*send).start()
            if h in OVER_PARTS:
                x_copy(o, h).start()
        if k == 0:
            own_arrived(2)
            load_offset.wait()
        if k == 1:
            swap_offset.wait()
            swap.wait()
        if k % PIECES == 0 and k > 0:
            tell(k // PIECES - 1)
        if k % PIECES == PIECES // 2:
            x_arrived(k // PIECES)

    def choose(step, low, high):
        if high - low == 1:
            talk(low)
            return
        mid = (low + high) // 2

        @pl.when(step < mid)
        def _():
            choose(step, low, mid)

        @pl.when(step >= mid)
        def _():
            choose(step, mid, high)

    def turn(step, carry):
        choose(step, 0, STEPS)
        compute(step)
        return carry

    lax.fori_loop(0, STEPS, turn, 0)
    tell(3)

    for count, sem in ((FETCH, yz_send), (OVER, x_send)):
        ref = gath.at[pl.ds(0, len(ARRIVALS) - 1), pl.ds(0, count)]
        pltpu.make_async_copy(ref, ref, sem).wait()
    pltpu.make_async_copy(got, got, a_recv).wait()
    pltpu.make_async_copy(got, got, a_send).wait()
    best = None
    for q in range(4):
        tiles = [got[i - 1] for i in range(q, len(ARRIVALS), 4) if i > 0]
        if q == 0:
            tiles.append(part[0])
        top = functools.reduce(jnp.maximum, tiles)[:, :, q * rows:(q + 1) * rows]
        best = top if best is None else jnp.maximum(best, top)
    nodev[node, :, :, 0:rows] = best
    for j in range(4):
        to = 4 * share + j

        @pl.when(to != node)
        def _():
            pltpu.make_async_remote_copy(
                src_ref=nodev.at[node], dst_ref=nodev.at[node], send_sem=b_send, recv_sem=b_recv,
                device_id=(to, cut), device_id_type=MESH,
            ).start()

    load_trans.wait()
    trans = weights[...]
    mixing = trans / jnp.sum(trans, axis=1, keepdims=True)
    holder = 1 - node // 4
    keeps = holder == core

    @pl.when(keeps)
    def _():
        ref = nodev.at[pl.ds(0, 3)]
        pltpu.make_async_copy(ref, ref, b_recv).wait()
        pltpu.make_async_copy(ref, ref, b_send).wait()

    @pl.when(jnp.logical_not(keeps))
    def _():
        ref = nodev.at[pl.ds(0, 4)]
        pltpu.make_async_copy(ref, ref, b_recv).wait()
        pltpu.make_async_copy(ref, ref, b_send).wait()

    known = jnp.concatenate(
        [nodev[2 * i + holder, m, :, 0:rows] for i in range(NX) for m in range(2)], axis=0
    )
    vals[...] = lax.dot_general(
        known.T, mixing, (((1,), (1,)), ((), ())),
        precision=lax.Precision.HIGHEST, preferred_element_type=jnp.float32,
    )
    out_ref[0] = vals[pl.ds(pl.multiple_of((node % 4) * 8, 8), 8), :]


def per_device(trial_states, cut_slopes, cut_intercepts, transition):
    node_local, cut_local, width = cut_slopes.shape
    rows = trial_states.shape[0]
    nodes = transition.shape[0]
    slope_rows = cut_slopes.reshape(node_local * cut_local, width)
    count = len(ARRIVALS)
    sems = pltpu.SemaphoreType.DMA
    return pl.pallas_call(
        kernel,
        out_shape=jax.ShapeDtypeStruct((1, rows // 8, nodes), jnp.float32),
        in_specs=[pl.BlockSpec(memory_space=pltpu.HBM)] * 4,
        out_specs=pl.BlockSpec(memory_space=pltpu.VMEM),
        scratch_shapes=[
            pltpu.VMEM((count, width // TILE, rows // 2, TILE), jnp.bfloat16),
            pltpu.VMEM((width // TILE, 2 * node_local * cut_local, TILE), jnp.bfloat16),
            pltpu.VMEM((2, node_local, cut_local), jnp.float32),
            pltpu.VMEM(transition.shape, jnp.float32),
            pltpu.VMEM((2, 4 * rows, node_local * cut_local), jnp.float32),
            pltpu.VMEM((count // 4, 2, node_local, 128), jnp.float32),
            pltpu.VMEM((count - 1, 2, node_local, 128), jnp.float32),
            pltpu.VMEM((8, 2, node_local, 128), jnp.float32),
            pltpu.VMEM((rows // 2, nodes), jnp.float32),
            sems((6,)),
            sems((2,)),
            sems((2,)),
            sems(()),
            sems((count - 1, len(PARTS))),
            sems(()),
            sems((count // 8,)),
            sems(()),
            sems(()),
            sems(()),
            sems(()),
        ],
        compiler_params=pltpu.CompilerParams(
            collective_id=0, has_side_effects=True, vmem_limit_bytes=40 * 1024 * 1024
        ),
        cost_estimate=pl.CostEstimate(
            flops=2 * 512 * 2048 * 4096, bytes_accessed=5 * 1024 * 1024, transcendentals=0
        ),
    )(*[
        pltpu.with_memory_space_constraint(v, pltpu.HBM)
        for v in (trial_states, slope_rows, cut_intercepts, transition)
    ])


def solution(mesh):
    return jax.shard_map(
        per_device,
        mesh=mesh,
        in_specs=(P("cut", None), P("node", "cut", None), P("node", "cut"), P()),
        out_specs=P("cut", "node", None),
        check_vma=False,
    )
```

```python
import functools

import jax
import jax.numpy as jnp
from jax import lax
from jax.experimental import pallas as pl
from jax.experimental.pallas import tpu as pltpu
from jax.sharding import PartitionSpec as P

MESH = pl.DeviceIdType.MESH

NY, NZ, NX = 4, 8, 4

TILE, OVER, MIDDLE = 128, 11, 10
FETCH = OVER + MIDDLE

PZ, MZ, PY, MY = (0, 1), (0, -1), (1, 0), (-1, 0)
LINKS = (PZ, MZ, PY, MY)

CROSS = {
    PZ: [(0, 1), (0, 2), (0, 3), (2, 1), (0, 4), (2, 2), (2, 3), (1, 4)],
    MZ: [(0, -1), (0, -2), (0, -3), (2, -1), (2, -2), (2, -3), (2, 4)],
    PY: [(1, 0), (2, 0), (1, 1), (1, -1), (1, 2), (1, -2), (1, 3), (1, -3)],
    MY: [(-1, 0), (-1, 1), (-1, -1), (-1, 2), (-1, -2), (-1, 3), (-1, -3), (-1, 4)],
}
PARTS = (0, 1, 2, 3)
OVER_PARTS = (0, 1)
SPANS = ((0, 6), (6, 5), (OVER, 5), (OVER + 5, 5))
TREES = (((1, 1), False), ((1, -1), False), ((1, 1), True), ((-1, 1), True))


def wrap(o):
    return (o[0] % NY, o[1] % NZ)


def arrival_links():
    links = {}
    for p, ((sy, sz), moved) in enumerate(TREES):
        for d, order in CROSS.items():
            for turn, o in enumerate(order):
                d_here, turn_here = d, turn
                if moved and o == (-1, 4):
                    d_here, turn_here = MZ, len(order)
                links[wrap((sy * o[0], sz * o[1])), p] = (sy * d_here[0], sz * d_here[1]), turn_here
    return links


def plan(window, span, delay):
    links = arrival_links()
    todo = {d: sorted((k for k in links if links[k][0] == d), key=lambda k: (links[k][1], k[1])) for d in LINKS}
    here = {((0, 0), h) for h in PARTS}
    free = dict.fromkeys(LINKS, 0.0)
    flying = dict.fromkeys(LINKS, 0)
    arrivals = []

    def issue(now):
        sends = []
        for d in LINKS:
            for o, h in list(todo[d]):
                source = wrap((o[0] - d[0], o[1] - d[1]))
                if flying[d] < window and (source, h) in here:
                    todo[d].remove((o, h))
                    flying[d] += 1
                    free[d] = max(free[d], now) + span
                    arrivals.append((free[d] + delay, len(arrivals), d, o, h))
                    sends.append((source, h, d))
        return sends

    first = issue(0.0)
    turns = []
    while len(turns) < len(arrivals):
        now, _, d, o, h = sorted(arrivals)[len(turns)]
        here.add((o, h))
        flying[d] -= 1
        turns.append((o, h, issue(now)))
    return first, turns


FIRST, TURNS = plan(window=4, span=1.1, delay=2.0)
DONE = {o: i for i, (o, _, _) in enumerate(TURNS)}
ARRIVALS = [(0, 0)] + sorted(DONE, key=DONE.get)
PLACE = {o: i for i, o in enumerate(ARRIVALS)}
PIECES = 4
PACE = (0, 4, 12, 14)
NEED = [1 + max(i for i, t in enumerate(TURNS) if PLACE[t[0]] < 8 * g + 8) for g in range(4)]
STEPS = 4 * PIECES


def handled(step):
    group, which = step // PIECES, step % PIECES
    if step < 0:
        return 0
    return NEED[group] + (NEED[min(group + 1, 3)] - NEED[group]) * PACE[which] // 16


def kernel(
    trial_ref, slope_ref, offset_ref, trans_ref, out_ref,
    gath, slopes, offset, weights, sums, part, got, nodev, vals,
    local_sem, swap_send, swap_recv, yz_send, yz_recv, x_send, x_recv, a_send, a_recv, b_send, b_recv,
):
    node = lax.axis_index("node")
    cut = lax.axis_index("cut")
    x, core = node // 2, node % 2
    y, z = cut // NZ, cut % NZ
    odd = x % 2
    sibling = x * 2 + 1 - core
    share = 1 - core
    tiles = gath.shape[1]
    own_rows = slope_ref.shape[0]
    rows = gath.shape[2]
    fetch_at = odd * OVER
    mine_at = odd * FETCH
    other_at = (1 - odd) * FETCH
    beside = {d: ((y + d[0] + NY) % NY) * NZ + (z + d[1] + NZ) % NZ for d in LINKS}

    def part_of(o, h):
        at, count = SPANS[h]
        return gath.at[PLACE[o], pl.ds(at + mine_at if h in OVER_PARTS else at, count)]

    def yz_copy(o, h, d):
        oc = wrap((o[0] + d[0], o[1] + d[1]))
        return pltpu.make_async_remote_copy(
            src_ref=part_of(o, h), dst_ref=part_of(oc, h),
            send_sem=yz_send, recv_sem=yz_recv.at[PLACE[oc] - 1, h],
            device_id=(node, beside[d]), device_id_type=MESH,
        )

    def yz_arrived(o, h):
        ref = part_of(o, h)
        pltpu.make_async_copy(ref, ref, yz_recv.at[PLACE[o] - 1, h]).wait()

    def x_copy(o, h):
        ref = part_of(o, h)
        to = ((x + (1 if (PLACE[o] + h) % 2 else NX - 1)) % NX) * 2 + core
        return pltpu.make_async_remote_copy(
            src_ref=ref, dst_ref=ref, send_sem=x_send, recv_sem=x_recv.at[PLACE[o] // 8],
            device_id=(to, cut), device_id_type=MESH,
        )

    def x_arrived(group):
        low = max(8 * group, 1)
        ref = gath.at[pl.ds(low, 8 * group + 8 - low), pl.ds(other_at, OVER)]
        pltpu.make_async_copy(ref, ref, x_recv.at[group]).wait()

    def product(group, at, count, owner):
        low = owner * own_rows
        left = [gath[pl.ds(8 * group, 8), at + k].reshape(8 * rows, TILE) for k in range(count)]
        right = [slopes[at + k, pl.ds(low, own_rows), :] for k in range(count)]
        return lax.dot_general(
            jnp.concatenate(left, axis=1), jnp.concatenate(right, axis=1), (((1,), (1,)), ((), ())),
            preferred_element_type=jnp.float32,
        )

    def compute(piece):
        group = lax.div(piece, PIECES)
        which = lax.rem(piece, PIECES)
        owner = lax.rem(core + which, 2)

        @pl.when(which < 2)
        def _():
            sums[owner] = product(group, fetch_at, FETCH, owner)

        @pl.when(which >= 2)
        def _():
            rest = product(group, other_at, OVER, owner)
            lane = lax.broadcasted_iota(jnp.int32, (8 * rows, TILE), 1)
            best = jnp.zeros((8 * rows, TILE), jnp.float32)
            for n in range(4):
                at = slice(n * 128, n * 128 + 128)
                total = sums[owner, :, at] + rest[:, at] + offset[owner, n:n + 1, :]
                best = jnp.where(lane == n, jnp.max(total, axis=1, keepdims=True), best)
            turned = best.T
            part[2 * group, owner] = turned[0:4, 0:128]
            part[2 * group + 1, owner] = turned[0:4, 128:256]

    def tell(group):
        for i in range(max(8 * group, 1), 8 * group + 8):
            o = ARRIVALS[i]
            owner = ((y - o[0] + NY) % NY) * NZ + (z - o[1] + NZ) % NZ
            pltpu.make_async_remote_copy(
                src_ref=part.at[i // 4], dst_ref=got.at[i - 1], send_sem=a_send, recv_sem=a_recv,
                device_id=(node, owner), device_id_type=MESH,
            ).start()

    def column(k):
        return pl.ds(pl.multiple_of(k * TILE, TILE), TILE)

    def own(k, sem):
        return pltpu.make_async_copy(
            trial_ref.at[pl.ds(share * rows, rows), column(k)], gath.at[0, k], sem
        )

    own_parts = ((mine_at, OVER, local_sem.at[0]), (OVER, MIDDLE, local_sem.at[4]), (other_at, OVER, local_sem.at[5]))

    def own_arrived(i):
        at, count, sem = own_parts[i]
        ref = gath.at[0, pl.ds(at, count)]
        pltpu.make_async_copy(ref, ref, sem).wait()

    def load(k):
        return pltpu.make_async_copy(
            slope_ref.at[:, column(k)], slopes.at[k, pl.ds(core * own_rows, own_rows)], local_sem.at[1]
        )

    loaded = slopes.at[:, pl.ds(core * own_rows, own_rows)]
    load_offset = pltpu.make_async_copy(offset_ref, offset.at[core], local_sem.at[2])
    load_trans = pltpu.make_async_copy(trans_ref, weights, local_sem.at[3])
    swap = pltpu.make_async_remote_copy(
        src_ref=loaded, dst_ref=loaded, send_sem=swap_send.at[0], recv_sem=swap_recv.at[0],
        device_id=(sibling, cut), device_id_type=MESH,
    )
    swap_offset = pltpu.make_async_remote_copy(
        src_ref=offset_ref, dst_ref=offset.at[core],
        send_sem=swap_send.at[1], recv_sem=swap_recv.at[1],
        device_id=(sibling, cut), device_id_type=MESH,
    )
    barrier = pltpu.get_barrier_semaphore()
    for d in LINKS:
        pl.semaphore_signal(barrier, inc=1, device_id=(node, beside[d]), device_id_type=MESH)
    for j in range(1, 8):
        pl.semaphore_signal(barrier, inc=1, device_id=((node + j) % 8, cut), device_id_type=MESH)
    for at, count, sem in own_parts:
        for k in range(count):
            own(at + k, sem).start()
    load_offset.start()
    load_trans.start()
    pl.semaphore_wait(barrier, 11)
    own_arrived(0)
    for o, h, d in FIRST:
        if h in OVER_PARTS:
            yz_copy(o, h, d).start()
    own_arrived(1)
    for o, h, d in FIRST:
        if h not in OVER_PARTS:
            yz_copy(o, h, d).start()
    swap_offset.start()
    for k in range(tiles):
        load(k).start()
    pltpu.make_async_copy(loaded, loaded, local_sem.at[1]).wait()
    swap.start()

    def talk(k):
        for o, h, sends in TURNS[handled(k - 1):handled(k)]:
            yz_arrived(o, h)
            for send in sends:
                yz_copy(*send).start()
            if h in OVER_PARTS:
                x_copy(o, h).start()
        if k == 0:
            own_arrived(2)
            load_offset.wait()
        if k == 1:
            swap_offset.wait()
            swap.wait()
        if k % PIECES == 0 and k > 0:
            tell(k // PIECES - 1)
        if k % PIECES == PIECES // 2:
            x_arrived(k // PIECES)

    def choose(step, low, high):
        if high - low == 1:
            talk(low)
            return
        mid = (low + high) // 2

        @pl.when(step < mid)
        def _():
            choose(step, low, mid)

        @pl.when(step >= mid)
        def _():
            choose(step, mid, high)

    def turn(step, carry):
        choose(step, 0, STEPS)
        compute(step)
        return carry

    lax.fori_loop(0, STEPS, turn, 0)
    tell(3)

    for count, sem in ((FETCH, yz_send), (OVER, x_send)):
        ref = gath.at[pl.ds(0, len(ARRIVALS) - 1), pl.ds(0, count)]
        pltpu.make_async_copy(ref, ref, sem).wait()
    pltpu.make_async_copy(got, got, a_recv).wait()
    pltpu.make_async_copy(got, got, a_send).wait()
    best = None
    for q in range(4):
        tiles = [got[i - 1] for i in range(q, len(ARRIVALS), 4) if i > 0]
        if q == 0:
            tiles.append(part[0])
        top = functools.reduce(jnp.maximum, tiles)[:, :, q * rows:(q + 1) * rows]
        best = top if best is None else jnp.maximum(best, top)
    nodev[node, :, :, 0:rows] = best
    for j in range(4):
        to = 4 * share + j

        @pl.when(to != node)
        def _():
            pltpu.make_async_remote_copy(
                src_ref=nodev.at[node], dst_ref=nodev.at[node], send_sem=b_send, recv_sem=b_recv,
                device_id=(to, cut), device_id_type=MESH,
            ).start()

    load_trans.wait()
    trans = weights[...]
    mixing = trans / jnp.sum(trans, axis=1, keepdims=True)
    holder = 1 - node // 4
    keeps = holder == core

    @pl.when(keeps)
    def _():
        ref = nodev.at[pl.ds(0, 3)]
        pltpu.make_async_copy(ref, ref, b_recv).wait()
        pltpu.make_async_copy(ref, ref, b_send).wait()

    @pl.when(jnp.logical_not(keeps))
    def _():
        ref = nodev.at[pl.ds(0, 4)]
        pltpu.make_async_copy(ref, ref, b_recv).wait()
        pltpu.make_async_copy(ref, ref, b_send).wait()

    known = jnp.concatenate(
        [nodev[2 * i + holder, m, :, 0:rows] for i in range(NX) for m in range(2)], axis=0
    )
    vals[...] = lax.dot_general(
        known.T, mixing, (((1,), (1,)), ((), ())),
        precision=lax.Precision.HIGHEST, preferred_element_type=jnp.float32,
    )
    out_ref[0] = vals[pl.ds(pl.multiple_of((node % 4) * 8, 8), 8), :]


def per_device(trial_states, cut_slopes, cut_intercepts, transition):
    node_local, cut_local, width = cut_slopes.shape
    rows = trial_states.shape[0]
    nodes = transition.shape[0]
    slope_rows = cut_slopes.reshape(node_local * cut_local, width)
    count = len(ARRIVALS)
    sems = pltpu.SemaphoreType.DMA
    return pl.pallas_call(
        kernel,
        out_shape=jax.ShapeDtypeStruct((1, rows // 8, nodes), jnp.float32),
        in_specs=[pl.BlockSpec(memory_space=pltpu.HBM)] * 4,
        out_specs=pl.BlockSpec(memory_space=pltpu.VMEM),
        scratch_shapes=[
            pltpu.VMEM((count, width // TILE, rows // 2, TILE), jnp.bfloat16),
            pltpu.VMEM((width // TILE, 2 * node_local * cut_local, TILE), jnp.bfloat16),
            pltpu.VMEM((2, node_local, cut_local), jnp.float32),
            pltpu.VMEM(transition.shape, jnp.float32),
            pltpu.VMEM((2, 4 * rows, node_local * cut_local), jnp.float32),
            pltpu.VMEM((count // 4, 2, node_local, 128), jnp.float32),
            pltpu.VMEM((count - 1, 2, node_local, 128), jnp.float32),
            pltpu.VMEM((8, 2, node_local, 128), jnp.float32),
            pltpu.VMEM((rows // 2, nodes), jnp.float32),
            sems((6,)),
            sems((2,)),
            sems((2,)),
            sems(()),
            sems((count - 1, len(PARTS))),
            sems(()),
            sems((count // 8,)),
            sems(()),
            sems(()),
            sems(()),
            sems(()),
        ],
        compiler_params=pltpu.CompilerParams(
            collective_id=0, has_side_effects=True, vmem_limit_bytes=40 * 1024 * 1024
        ),
        cost_estimate=pl.CostEstimate(
            flops=2 * 512 * 2048 * 4096, bytes_accessed=5 * 1024 * 1024, transcendentals=0
        ),
    )(*[
        pltpu.with_memory_space_constraint(v, pltpu.HBM)
        for v in (trial_states, slope_rows, cut_intercepts, transition)
    ])


def solution(mesh):
    return jax.shard_map(
        per_device,
        mesh=mesh,
        in_specs=(P("cut", None), P("node", "cut", None), P("node", "cut"), P()),
        out_specs=P("cut", "node", None),
        check_vma=False,
    )
```
